32 devices in a mesh: groups: 2 (over x), ha: 16 (over z, y, core).
Axes of the slice: x: 2, y: 2, z: 4, core: 2. Of those that a mesh axis runs over, the one named last changes fastest.
Arguments:
- coarse: bfloat16 [64, 8, 16, 16], P(None, 'groups', 'ha'), parts along dimension 1, may hold values from -6 to 6
- skip: bfloat16 [32, 16, 32, 32], P(None, 'groups', 'ha'), parts along dimension 1, may hold values from -6 to 6
- up_weight: bfloat16 [2, 2, 2, 64, 64], replicated, may hold values from -0.75 to 0.75
- up_bias: float32 [64], replicated, may hold values from -3 to 3
- conv1_weight: bfloat16 [3, 3, 3, 32, 96], replicated, may hold values from -0.125 to 0.125
- conv1_bias: float32 [32], replicated, may hold values from -3 to 3
- conv2_weight: bfloat16 [3, 3, 3, 32, 32], replicated, may hold values from -0.21875 to 0.21875
- conv2_bias: float32 [32], replicated, may hold values from -3 to 3
Outputs:
- decoded: bfloat16 [32, 16, 32, 32], P(None, 'groups', 'ha'), parts along dimension 1
The draws below stay inside these ranges and needn't reach their ends.
There are 2 independent parts, one for each index of `groups`. The reference program is written for one: setup_inputs(seed, part) draws one part's arguments, and reference() takes and returns one part's arrays. A program takes and returns all parts, laid end to end along the dimension named above; an argument that names none is the same for every part. Nothing has to cross between parts.
All inputs are finite; a program needn't handle non-finite values.
Results may differ from the reference program's by a relative error of at most 0.005.
Values may be sent and summed in bfloat16 or wider, within the bound.
A program may use at most 64 MiB of HBM per device.

```python
import jax
import jax.numpy as jnp
from jax import lax

CUP = 64
SKIPC = 32
OUTC = 32
CD = 4
CH = 16
CW = 16
FD = 8
FH = 32
FW = 32


def levels(rng, shape, cuts, low, high):
    def one(axis_at, parts):
        steps = jax.random.uniform(jax.random.fold_in(jax.random.fold_in(rng, 6), axis_at), (parts,), jnp.float32, low / len(cuts), high / len(cuts))
        return jnp.repeat(jnp.exp(steps), shape[axis_at] // parts).reshape((-1,) + (1,) * (len(shape) - axis_at - 1))

    level = one(*cuts[0])
    for cut in cuts[1:]:
        level = level * one(*cut)
    return level


def centred(rng, extent, width, reach, split=(), kind=jnp.bfloat16):
    drawn = jax.random.normal(rng, extent, jnp.float32) * width
    if len(split) > 0:
        drawn = levels(rng, extent, split, -0.22, 0.18) * drawn
    return jnp.clip(drawn, min=-reach, max=reach).astype(kind)


def setup_inputs(seed: int = 0, part: int = 0) -> dict:
    key_of = jax.random.split(jax.random.key(seed), 9)
    own_keys = jax.random.split(jax.random.fold_in(key_of[8], part), 9)
    coarse = centred(own_keys[0], (CUP, CD, CW, CH), 1.0, 6.0, ((2, 16),))
    skip = centred(own_keys[1], (SKIPC, FD, FH, FW), 1.0, 6.0, ((2, 16),))
    up_weight = centred(key_of[2], (2, 2, 2, CUP, CUP), CUP ** -0.5, 0.75)
    up_bias = centred(key_of[3], (CUP,), 0.5, 3.0, (), jnp.float32)
    conv1_weight = centred(key_of[4], (3, 3, 3, OUTC, CUP + SKIPC), (27 * (CUP + SKIPC)) ** -0.5, 0.125)
    conv1_bias = centred(key_of[5], (OUTC,), 0.5, 3.0, (), jnp.float32)
    conv2_weight = centred(key_of[6], (3, 3, 3, OUTC, OUTC), (27 * OUTC) ** -0.5, 0.21875)
    conv2_bias = centred(key_of[7], (OUTC,), 0.5, 3.0, (), jnp.float32)
    return dict(coarse=coarse, skip=skip, up_weight=up_weight, up_bias=up_bias, conv1_weight=conv1_weight, conv1_bias=conv1_bias, conv2_weight=conv2_weight, conv2_bias=conv2_bias)


def upsample_slab(slab, weight, bias):
    values = jnp.einsum("abcoi,iwh->oahbwc", weight, slab.astype(jnp.float32), precision=lax.Precision.HIGHEST)
    channels = weight.shape[3]
    values = values.reshape(channels, 2, 2 * slab.shape[2], 2 * slab.shape[1])
    return (values + bias[:, None, None, None]).astype(jnp.bfloat16)


def conv_layer(inputs, weight, bias):
    padded = jnp.pad(inputs, ((0, 0), (1, 1), (1, 1), (1, 1)))
    kernel = weight.astype(jnp.float32)

    def one_slice(depth):
        slab = lax.dynamic_slice_in_dim(padded, depth, 3, 1).astype(jnp.float32)
        result = lax.conv_general_dilated(slab[None], kernel, (1, 1, 1), "VALID",
                                          dimension_numbers=("NCDHW", "DHWOI", "NCDHW"),
                                          precision=lax.Precision.HIGHEST)
        return jnp.maximum(result[0, :, 0] + bias[:, None, None], 0.0).astype(jnp.bfloat16)

    slices = lax.map(one_slice, jnp.arange(inputs.shape[1], dtype=jnp.int32))
    return jnp.moveaxis(slices, 0, 1)


def reference(coarse, skip, up_weight, up_bias, conv1_weight, conv1_bias, conv2_weight, conv2_bias):
    weight = up_weight.astype(jnp.float32)
    upsampled = lax.map(lambda slab: upsample_slab(slab, weight, up_bias), jnp.moveaxis(coarse, 1, 0))
    upsampled = jnp.moveaxis(upsampled, 0, 1)
    upsampled = upsampled.reshape(CUP, FD, FH, FW)
    joined = jnp.concatenate([upsampled, skip], axis=0)
    hidden = conv_layer(joined, conv1_weight, conv1_bias)
    return conv_layer(hidden, conv2_weight, conv2_bias)
```

```python
import functools

import jax
import jax.numpy as jnp
from jax import lax
from jax.experimental import pallas as pl
from jax.experimental.pallas import tpu as pltpu
from jax.sharding import PartitionSpec as P

VMEM_BUDGET = 40 * 1024 * 1024
MARGIN = 2
ROW_TILE = 16


def with_halo(array, sides, width):
    for axis, dim in sides:
        count, length = (lax.axis_size(axis), array.shape[dim])
        up = [(i, (i + 1) % count) for i in range(count - 1)]
        down = [(j, i) for i, j in up]
        last = lax.slice_in_dim(array, length - width, length, axis=dim)
        first = lax.slice_in_dim(array, 0, width, axis=dim)
        before = lax.ppermute(last, axis, up)
        after = lax.ppermute(first, axis, down)
        array = jnp.concatenate([before, array, after], axis=dim)
    return array


def upsample(inputs, weight, bias):
    values = jnp.einsum("abcoi,idpq->odapbqc", weight, inputs, preferred_element_type=jnp.float32)
    channels = weight.shape[3]
    values = values.reshape(channels, 2 * inputs.shape[1], 2 * inputs.shape[2], 2 * inputs.shape[3])
    return (values + bias[:, None, None, None]).astype(jnp.bfloat16)


def convolve(inputs, weight, bias):
    result = lax.conv_general_dilated(
        inputs[None],
        weight,
        (1, 1, 1),
        ((1, 1), (0, 0), (1, 1)),
        dimension_numbers=("NCDHW", "DHWOI", "NCDHW"),
        preferred_element_type=jnp.float32,
    )[0]
    return jnp.maximum(result + bias[:, None, None, None], 0.0).astype(jnp.bfloat16)


def inside_rows(height_rows, margin_rows):
    row_index = (
        lax.axis_index("ha") * height_rows
        - margin_rows
        + jnp.arange(height_rows + 2 * margin_rows, dtype=jnp.int32)
    )
    return (row_index >= 0) & (row_index < lax.axis_size("ha") * height_rows)


def large_body(coarse, skip, up_weight, up_bias, conv1_weight, conv1_bias, conv2_weight, conv2_bias):
    margin_rows = 2
    height_rows = skip.shape[2]
    local_fine = upsample(coarse, jnp.transpose(up_weight, (0, 2, 1, 3, 4)), up_bias)
    moved = lax.all_to_all(local_fine, "ha", split_axis=3, concat_axis=2, tiled=True)
    joined = jnp.concatenate([jnp.swapaxes(moved, 2, 3), skip], axis=0)
    padded = with_halo(joined, (("ha", 2),), margin_rows)
    widened = convolve(padded, conv1_weight, conv1_bias)
    inside = inside_rows(height_rows, 1)
    padded_hidden = jnp.where(inside[None, None, :, None], widened, jnp.zeros((), jnp.bfloat16))
    return convolve(padded_hidden, conv2_weight, conv2_bias)


def iota(shape, dim):
    return lax.broadcasted_iota(jnp.int32, shape, dim)


def column(row):
    size = row.shape[1]
    same = iota((size, size), 0) == iota((size, size), 1)
    return jnp.sum(jnp.where(same, row, 0.0), axis=1, keepdims=True)


def one_hot(wanted, count):
    return jnp.where(iota((wanted.shape[0], count), 1) == wanted, 1.0, 0.0).astype(jnp.bfloat16)


def nt_dot(a, b):
    return lax.dot_general(a, b, (((1,), (1,)), ((), ())), preferred_element_type=jnp.float32)


def nn_dot(a, b):
    return lax.dot_general(a, b, (((1,), (0,)), ((), ())), preferred_element_type=jnp.float32)


def shifted_sum(weights, inputs_ref, rows_out, plane, fine_w, fine_d, outc):
    parts = [[None] * 9 for _ in range(rows_out)]
    for y in range(rows_out + 2):
        taps = nn_dot(weights, inputs_ref[:, y * plane : (y + 1) * plane])
        for q in range(3):
            t = y - q
            if 0 <= t < rows_out:
                for p in range(3):
                    for r in range(3):
                        at = ((p * 3 + q) * 3 + r) * outc
                        term = taps[at : at + outc]
                        old = parts[t][p * 3 + r]
                        parts[t][p * 3 + r] = term if old is None else old + term
    lane = iota((1, plane), 1)
    x, z = lax.rem(lane, fine_w), lax.div(lane, fine_w)
    results = []
    for t in range(rows_out):
        planes = []
        for p in range(3):
            before, here, after = parts[t][3 * p : 3 * p + 3]
            here = here + jnp.where(x > 0, pltpu.roll(before, 1, 1), 0.0)
            here = here + jnp.where(x < fine_w - 1, pltpu.roll(after, plane - 1, 1), 0.0)
            planes.append(here)
        total = planes[1]
        total = total + jnp.where(z > 0, pltpu.roll(planes[0], fine_w, 1), 0.0)
        total = total + jnp.where(z < fine_d - 1, pltpu.roll(planes[2], plane - fine_w, 1), 0.0)
        results.append(total)
    return results


def kernel(
    n, depth, width, height, slab,
    coarse_ref, skip_ref, upw_hbm, upb_ref, w1_hbm, b1_ref, w2_hbm, b2_ref,
    out_ref,
    outgoing, incoming, joined, hidden, upw_ref, w1_ref, w2_ref,
    coarse_send, coarse_recv, skip_send, skip_recv, load_sem,
):
    me = lax.axis_index("ha")
    cup = upw_ref.shape[1]
    outc, skipc = out_ref.shape[0], skip_ref.shape[0]
    near = height // n
    own = 2 * near
    local_w = width // n
    fine_w, fine_d = 2 * width, 2 * depth
    plane = fine_w * fine_d

    barrier = pltpu.get_barrier_semaphore()
    for k in range(1, n):
        pl.semaphore_signal(
            barrier, inc=1, device_id={"ha": lax.rem(me + k, n)}, device_id_type=pl.DeviceIdType.MESH
        )
    loads = [
        pltpu.make_async_copy(src, dst, load_sem.at[i])
        for i, (src, dst) in enumerate(((upw_hbm, upw_ref), (w1_hbm, w1_ref), (w2_hbm, w2_ref)))
    ]
    for load in loads:
        load.start()
    own_skip = pltpu.make_async_copy(
        skip_ref, joined.at[pl.ds(cup, skipc), pl.ds(MARGIN * plane, own * plane)], load_sem.at[3]
    )
    own_skip.start()

    at = iota((n * slab, 1), 0)
    to, slot = lax.div(at, slab), lax.rem(at, slab)
    row = to * near - 1 + lax.div(slot, depth * local_w)
    wanted = (lax.rem(lax.div(slot, local_w), depth) * local_w + lax.rem(slot, local_w)) * height + row
    real = (row >= 0) & (row < height) & (slot < (near + 2) * depth * local_w)
    picked = nn_dot(one_hot(jnp.where(real, wanted, -1), depth * local_w * height), coarse_ref[...])
    outgoing[...] = picked.astype(jnp.bfloat16).reshape(n, slab, cup)

    pl.semaphore_wait(barrier, n - 1)

    edge = MARGIN * plane
    above = pltpu.make_async_remote_copy(
        src_ref=skip_ref.at[:, pl.ds(0, edge)],
        dst_ref=joined.at[pl.ds(cup, skipc), pl.ds((MARGIN + own) * plane, edge)],
        send_sem=skip_send.at[0], recv_sem=skip_recv.at[0],
        device_id={"ha": jnp.maximum(me - 1, 0)}, device_id_type=pl.DeviceIdType.MESH,
    )
    below = pltpu.make_async_remote_copy(
        src_ref=skip_ref.at[:, pl.ds((own - MARGIN) * plane, edge)],
        dst_ref=joined.at[pl.ds(cup, skipc), pl.ds(0, edge)],
        send_sem=skip_send.at[1], recv_sem=skip_recv.at[1],
        device_id={"ha": jnp.minimum(me + 1, n - 1)}, device_id_type=pl.DeviceIdType.MESH,
    )
    for k in range(1, n):
        to = lax.rem(me + (n // 2 + k - 1) % (n - 1) + 1, n)
        pltpu.make_async_remote_copy(
            src_ref=outgoing.at[to], dst_ref=incoming.at[me],
            send_sem=coarse_send, recv_sem=coarse_recv,
            device_id={"ha": to}, device_id_type=pl.DeviceIdType.MESH,
        ).start()
    pl.when(me > 0)(above.start)
    pl.when(me < n - 1)(below.start)
    pltpu.make_async_copy(outgoing.at[me], incoming.at[me], coarse_recv).start()

    at = iota(((near + 2) * plane, 1), 0)
    h, z, w = lax.div(at, plane), lax.rem(lax.div(at, fine_w), fine_d), lax.div(lax.rem(at, fine_w), 2)
    source = one_hot(
        lax.div(w, local_w) * slab + (h * depth + lax.div(z, 2)) * local_w + lax.rem(w, local_w), n * slab
    )
    lane = iota((1, plane), 1)
    odd_x = lax.rem(lane, 2) == 1
    odd_z = lax.rem(lax.div(lane, fine_w), 2) == 1
    up_bias, bias1, bias2 = column(upb_ref[...]), column(b1_ref[...]), column(b2_ref[...])

    def inside(row):
        return (me * own + row >= 0) & (me * own + row < n * own)

    @pl.when(me == 0)
    def _():
        joined[cup:, : MARGIN * plane] = jnp.zeros((skipc, MARGIN * plane), jnp.bfloat16)

    @pl.when(me == n - 1)
    def _():
        joined[cup:, (MARGIN + own) * plane :] = jnp.zeros((skipc, MARGIN * plane), jnp.bfloat16)

    for load in loads:
        load.wait()
    pltpu.make_async_copy(incoming, incoming, coarse_recv).wait()

    spread = nn_dot(source, incoming[...].reshape(n * slab, cup)).astype(jnp.bfloat16)
    for h in range(near + 2):
        taps = nt_dot(upw_ref[...], spread[h * plane : (h + 1) * plane])
        for b in range(2):
            def tap(a, c):
                at = ((a * 2 + b) * 2 + c) * cup
                return taps[at : at + cup]

            even = jnp.where(odd_x, tap(0, 1), tap(0, 0))
            odd = jnp.where(odd_x, tap(1, 1), tap(1, 0))
            values = jnp.where(odd_z, odd, even) + up_bias
            y = 2 * h + b
            values = jnp.where(inside(y - MARGIN), values, 0.0)
            joined[:cup, y * plane : (y + 1) * plane] = values.astype(jnp.bfloat16)

    own_skip.wait()
    pl.when(me < n - 1)(above.wait_recv)
    pl.when(me > 0)(below.wait_recv)

    for t, total in enumerate(shifted_sum(w1_ref[...], joined, own + 2, plane, fine_w, fine_d, outc)):
        values = jnp.where(inside(t - 1), jnp.maximum(total + bias1, 0.0), 0.0)
        hidden[:, t * plane : (t + 1) * plane] = values.astype(jnp.bfloat16)
    for t, total in enumerate(shifted_sum(w2_ref[...], hidden, own, plane, fine_w, fine_d, outc)):
        out_ref[:, t * plane : (t + 1) * plane] = jnp.maximum(total + bias2, 0.0).astype(jnp.bfloat16)

    pl.when(me > 0)(above.wait_send)
    pl.when(me < n - 1)(below.wait_send)
    pltpu.make_async_copy(outgoing.at[pl.ds(0, n - 1)], incoming.at[pl.ds(0, n - 1)], coarse_send).wait()


def body(coarse, skip, up_weight, up_bias, conv1_weight, conv1_bias, conv2_weight, conv2_bias):
    n = lax.axis_size("ha")
    cup, depth, local_w, height = coarse.shape
    skipc, fine_d, own, fine_w = skip.shape
    outc = conv1_weight.shape[3]
    near = height // n
    width = local_w * n
    plane = fine_d * fine_w
    slab = -(-((near + 2) * depth * local_w) // ROW_TILE) * ROW_TILE
    taps = 27 * outc * plane * 4
    need = (near + 2) * plane * (n * slab * 6 + 4 * 8 * cup) + (own + 4) * taps
    if need > VMEM_BUDGET or plane % 128 or near < 1 or own < MARGIN:
        return large_body(
            coarse, skip, up_weight, up_bias, conv1_weight, conv1_bias, conv2_weight, conv2_bias
        )
    vmem, hbm = pl.BlockSpec(memory_space=pltpu.VMEM), pl.BlockSpec(memory_space=pl.ANY)
    upw = up_weight.reshape(8 * cup, cup)
    w1 = conv1_weight.reshape(27 * outc, cup + skipc)
    w2 = conv2_weight.reshape(27 * outc, outc)
    out = pl.pallas_call(
        functools.partial(kernel, n, depth, width, height, slab),
        out_shape=jax.ShapeDtypeStruct((outc, own * plane), jnp.bfloat16),
        in_specs=[vmem, vmem, hbm, vmem, hbm, vmem, hbm, vmem],
        out_specs=vmem,
        scratch_shapes=[
            pltpu.VMEM((n, slab, cup), jnp.bfloat16),
            pltpu.VMEM((n, slab, cup), jnp.bfloat16),
            pltpu.VMEM((cup + skipc, (own + 2 * MARGIN) * plane), jnp.bfloat16),
            pltpu.VMEM((outc, (own + 2) * plane), jnp.bfloat16),
            pltpu.VMEM(upw.shape, jnp.bfloat16),
            pltpu.VMEM(w1.shape, jnp.bfloat16),
            pltpu.VMEM(w2.shape, jnp.bfloat16),
            pltpu.SemaphoreType.DMA,
            pltpu.SemaphoreType.DMA,
            pltpu.SemaphoreType.DMA((2,)),
            pltpu.SemaphoreType.DMA((2,)),
            pltpu.SemaphoreType.DMA((4,)),
        ],
        compiler_params=pltpu.CompilerParams(
            collective_id=0, has_side_effects=True, vmem_limit_bytes=VMEM_BUDGET
        ),
    )(
        jnp.transpose(coarse, (1, 2, 3, 0)).reshape(depth * local_w * height, cup),
        jnp.swapaxes(skip, 1, 2).reshape(skipc, own * plane),
        upw,
        up_bias[None],
        w1,
        conv1_bias[None],
        w2,
        conv2_bias[None],
    )
    return jnp.swapaxes(out.reshape(outc, own, fine_d, fine_w), 1, 2)


def solution(mesh):
    return jax.shard_map(
        body,
        mesh=mesh,
        in_specs=(
            P(None, "groups", "ha", None),
            P(None, "groups", "ha", None),
            P(),
            P(),
            P(),
            P(),
            P(),
            P(),
        ),
        out_specs=P(None, "groups", "ha", None),
        check_vma=False,
    )
```

```python
import functools

import jax
import jax.numpy as jnp
from jax import lax
from jax.experimental import pallas as pl
from jax.experimental.pallas import tpu as pltpu
from jax.sharding import PartitionSpec as P

VMEM_BUDGET = 40 * 1024 * 1024
VMEM_LIMIT = 60 * 1024 * 1024
MARGIN = 2
ROW_TILE = 16


def with_halo(array, sides, width):
    for axis, dim in sides:
        count, length = (lax.axis_size(axis), array.shape[dim])
        up = [(i, (i + 1) % count) for i in range(count - 1)]
        down = [(j, i) for i, j in up]
        last = lax.slice_in_dim(array, length - width, length, axis=dim)
        first = lax.slice_in_dim(array, 0, width, axis=dim)
        before = lax.ppermute(last, axis, up)
        after = lax.ppermute(first, axis, down)
        array = jnp.concatenate([before, array, after], axis=dim)
    return array


def upsample(inputs, weight, bias):
    values = jnp.einsum("abcoi,idpq->odapbqc", weight, inputs, preferred_element_type=jnp.float32)
    channels = weight.shape[3]
    values = values.reshape(channels, 2 * inputs.shape[1], 2 * inputs.shape[2], 2 * inputs.shape[3])
    return (values + bias[:, None, None, None]).astype(jnp.bfloat16)


def convolve(inputs, weight, bias):
    result = lax.conv_general_dilated(
        inputs[None],
        weight,
        (1, 1, 1),
        ((1, 1), (0, 0), (1, 1)),
        dimension_numbers=("NCDHW", "DHWOI", "NCDHW"),
        preferred_element_type=jnp.float32,
    )[0]
    return jnp.maximum(result + bias[:, None, None, None], 0.0).astype(jnp.bfloat16)


def inside_rows(height_rows, margin_rows):
    row_index = (
        lax.axis_index("ha") * height_rows
        - margin_rows
        + jnp.arange(height_rows + 2 * margin_rows, dtype=jnp.int32)
    )
    return (row_index >= 0) & (row_index < lax.axis_size("ha") * height_rows)


def large_body(coarse, skip, up_weight, up_bias, conv1_weight, conv1_bias, conv2_weight, conv2_bias):
    margin_rows = 2
    height_rows = skip.shape[2]
    local_fine = upsample(coarse, jnp.transpose(up_weight, (0, 2, 1, 3, 4)), up_bias)
    moved = lax.all_to_all(local_fine, "ha", split_axis=3, concat_axis=2, tiled=True)
    joined = jnp.concatenate([jnp.swapaxes(moved, 2, 3), skip], axis=0)
    padded = with_halo(joined, (("ha", 2),), margin_rows)
    widened = convolve(padded, conv1_weight, conv1_bias)
    inside = inside_rows(height_rows, 1)
    padded_hidden = jnp.where(inside[None, None, :, None], widened, jnp.zeros((), jnp.bfloat16))
    return convolve(padded_hidden, conv2_weight, conv2_bias)


def iota(shape, dim):
    return lax.broadcasted_iota(jnp.int32, shape, dim)


def column(row):
    size = row.shape[1]
    same = iota((size, size), 0) == iota((size, size), 1)
    return jnp.sum(jnp.where(same, row, 0.0), axis=1, keepdims=True)


def as_bits(mask):
    return jnp.where(mask, 1.0, 0.0).astype(jnp.bfloat16)


def one_hot(wanted, count):
    return as_bits(iota((wanted.shape[0], count), 1) == wanted)


def nt_dot(a, b):
    return lax.dot_general(a, b, (((1,), (1,)), ((), ())), preferred_element_type=jnp.float32)


def nn_dot(a, b):
    return lax.dot_general(a, b, (((1,), (0,)), ((), ())), preferred_element_type=jnp.float32)


def same_depth(channels, own, fine_d, fine_w):
    row = iota((channels * fine_d * own, 1), 0)
    lane = iota((1, fine_d * fine_w), 1)
    return lax.rem(lax.div(row, own), fine_d) == lax.div(lane, fine_w)


def width_tiles(fine_d, fine_w):
    shape = (fine_w, fine_d * fine_w)
    return as_bits(lax.rem(iota(shape, 1), fine_w) == iota(shape, 0))


def planes_of(rows, channels, own, fine_d, fine_w):
    wide = nn_dot(rows, width_tiles(fine_d, fine_w))
    wide = jnp.where(same_depth(channels, own, fine_d, fine_w), wide, 0.0).astype(jnp.bfloat16)
    at = iota((1, rows.shape[0]), 1)
    goal = lax.rem(at, own) * channels + lax.div(at, own * fine_d)
    return nn_dot(as_bits(iota((own * channels, 1), 0) == goal), wide).astype(jnp.bfloat16)


def rows_of(planes, channels, own, fine_d, fine_w):
    at = iota((channels * fine_d * own, 1), 0)
    goal = lax.rem(at, own) * channels + lax.div(at, own * fine_d)
    wide = nn_dot(one_hot(goal, own * channels), planes)
    wide = jnp.where(same_depth(channels, own, fine_d, fine_w), wide, 0.0).astype(jnp.bfloat16)
    return nt_dot(wide, width_tiles(fine_d, fine_w)).astype(jnp.bfloat16)


def stack_height_taps(weights, outc):
    block = 3 * outc
    bands = []
    for p in range(3):
        taps = [weights[(p * 3 + q) * block : (p * 3 + q + 1) * block] for q in range(3)]
        bands.append(jnp.concatenate(taps, axis=1))
    return jnp.concatenate(bands, axis=0)


def store_stacked(stacked_ref, values, y, rows_out, channels, first, plane):
    for q in range(3):
        t = y - q
        if 0 <= t < rows_out:
            at = q * channels + first
            stacked_ref[at : at + values.shape[0], t * plane : (t + 1) * plane] = values


def convolved_row(weights, inputs, fine_w, fine_d, outc):
    plane = fine_w * fine_d
    taps = nn_dot(weights, inputs)
    lane = iota((1, plane), 1)
    x, z = lax.rem(lane, fine_w), lax.div(lane, fine_w)
    planes = []
    for p in range(3):
        before, here, after = (taps[(p * 3 + r) * outc : (p * 3 + r + 1) * outc] for r in range(3))
        here = here + jnp.where(x > 0, pltpu.roll(before, 1, 1), 0.0)
        here = here + jnp.where(x < fine_w - 1, pltpu.roll(after, plane - 1, 1), 0.0)
        planes.append(here)
    total = planes[1]
    total = total + jnp.where(z > 0, pltpu.roll(planes[0], fine_w, 1), 0.0)
    return total + jnp.where(z < fine_d - 1, pltpu.roll(planes[2], plane - fine_w, 1), 0.0)


def kernel(
    n, depth, width, height, slab,
    coarse_hbm, skip_hbm, upw_hbm, upb_hbm, w1_hbm, b1_hbm, w2_hbm, b2_hbm,
    out_ref,
    coarse_ref, skip_ref, upw_ref, upb_ref, w1_ref, b1_ref, w2_ref, b2_ref,
    outgoing, incoming, mine, theirs, joined, hidden,
    coarse_send, coarse_recv, skip_send, skip_recv, load_sem,
):
    me = lax.axis_index("ha")
    cup, outc = upw_ref.shape[1], w2_ref.shape[1]
    skipc = w1_ref.shape[1] - cup
    near = height // n
    own = 2 * near
    local_w = width // n
    fine_w, fine_d = 2 * width, 2 * depth
    plane = fine_w * fine_d
    joint = cup + skipc

    operands = (
        (coarse_hbm, coarse_ref), (skip_hbm, skip_ref), (w1_hbm, w1_ref), (w2_hbm, w2_ref),
        (upw_hbm, upw_ref), (upb_hbm, upb_ref), (b1_hbm, b1_ref), (b2_hbm, b2_ref),
    )
    loads = [pltpu.make_async_copy(src, dst, load_sem.at[i]) for i, (src, dst) in enumerate(operands)]
    for load in loads[:2]:
        load.start()
    barrier = pltpu.get_barrier_semaphore()
    for k in range(1, n):
        pl.semaphore_signal(
            barrier, inc=1, device_id={"ha": lax.rem(me + k, n)}, device_id_type=pl.DeviceIdType.MESH
        )
    for load in loads[2:]:
        load.start()

    at = iota((n * slab, 1), 0)
    to, slot = lax.div(at, slab), lax.rem(at, slab)
    row = to * near - 1 + lax.div(slot, depth * local_w)
    wanted = (lax.rem(lax.div(slot, local_w), depth) * local_w + lax.rem(slot, local_w)) * height + row
    real = (row >= 0) & (row < height) & (slot < (near + 2) * depth * local_w)
    pick = one_hot(jnp.where(real, wanted, -1), depth * local_w * height)
    loads[0].wait()
    outgoing[...] = nn_dot(pick, coarse_ref[...]).astype(jnp.bfloat16).reshape(n, slab, cup)
    loads[1].wait()
    mine[...] = planes_of(skip_ref[...], skipc, own, fine_d, fine_w)

    @pl.when(me == 0)
    def _():
        theirs[0] = jnp.zeros(theirs.shape[1:], theirs.dtype)

    @pl.when(me == n - 1)
    def _():
        theirs[1] = jnp.zeros(theirs.shape[1:], theirs.dtype)

    pl.semaphore_wait(barrier, n - 1)

    edge = MARGIN * skipc
    for k in range(1, n):
        to = lax.rem(me + (n // 2 + k - 1) % (n - 1) + 1, n)
        pltpu.make_async_remote_copy(
            src_ref=outgoing.at[to], dst_ref=incoming.at[me],
            send_sem=coarse_send, recv_sem=coarse_recv,
            device_id={"ha": to}, device_id_type=pl.DeviceIdType.MESH,
        ).start()
    upward = pltpu.make_async_remote_copy(
        src_ref=mine.at[pl.ds(0, edge)], dst_ref=theirs.at[1],
        send_sem=skip_send.at[0], recv_sem=skip_recv.at[0],
        device_id={"ha": jnp.maximum(me - 1, 0)}, device_id_type=pl.DeviceIdType.MESH,
    )
    downward = pltpu.make_async_remote_copy(
        src_ref=mine.at[pl.ds((own - MARGIN) * skipc, edge)], dst_ref=theirs.at[0],
        send_sem=skip_send.at[1], recv_sem=skip_recv.at[1],
        device_id={"ha": jnp.minimum(me + 1, n - 1)}, device_id_type=pl.DeviceIdType.MESH,
    )
    pl.when(me > 0)(upward.start)
    pl.when(me < n - 1)(downward.start)
    pltpu.make_async_copy(outgoing.at[me], incoming.at[me], coarse_recv).start()

    at = iota(((near + 2) * plane, 1), 0)
    h, z, w = lax.div(at, plane), lax.rem(lax.div(at, fine_w), fine_d), lax.div(lax.rem(at, fine_w), 2)
    source = one_hot(
        lax.div(w, local_w) * slab + (h * depth + lax.div(z, 2)) * local_w + lax.rem(w, local_w), n * slab
    )
    lane = iota((1, plane), 1)
    odd_x = lax.rem(lane, 2) == 1
    odd_z = lax.rem(lax.div(lane, fine_w), 2) == 1
    for load in loads[2:]:
        load.wait()
    weights1 = stack_height_taps(w1_ref[...], outc)
    weights2 = stack_height_taps(w2_ref[...], outc)
    up_bias, bias1, bias2 = column(upb_ref[...]), column(b1_ref[...]), column(b2_ref[...])

    def inside(row):
        return (me * own + row >= 0) & (me * own + row < n * own)

    for y in range(own):
        store_stacked(joined, mine[y * skipc : (y + 1) * skipc], y + MARGIN, own + 2, joint, cup, plane)
    pl.when(me < n - 1)(upward.wait_recv)
    pl.when(me > 0)(downward.wait_recv)
    for y in range(MARGIN):
        rows = slice(y * skipc, (y + 1) * skipc)
        store_stacked(joined, theirs[0, rows], y, own + 2, joint, cup, plane)
        store_stacked(joined, theirs[1, rows], y + MARGIN + own, own + 2, joint, cup, plane)
    pltpu.make_async_copy(incoming, incoming, coarse_recv).wait()

    spread = nn_dot(source, incoming[...].reshape(n * slab, cup)).astype(jnp.bfloat16)
    for h in range(near + 2):
        taps = nt_dot(upw_ref[...], spread[h * plane : (h + 1) * plane])
        for b in range(2):
            def tap(a, c):
                at = ((a * 2 + b) * 2 + c) * cup
                return taps[at : at + cup]

            even = jnp.where(odd_x, tap(0, 1), tap(0, 0))
            odd = jnp.where(odd_x, tap(1, 1), tap(1, 0))
            values = jnp.where(odd_z, odd, even) + up_bias
            y = 2 * h + b
            values = jnp.where(inside(y - MARGIN), values, 0.0).astype(jnp.bfloat16)
            store_stacked(joined, values, y, own + 2, joint, 0, plane)

    for t in range(own + 2):
        total = convolved_row(weights1, joined[:, t * plane : (t + 1) * plane], fine_w, fine_d, outc)
        values = jnp.where(inside(t - 1), jnp.maximum(total + bias1, 0.0), 0.0).astype(jnp.bfloat16)
        store_stacked(hidden, values, t, own, outc, 0, plane)
    outs = []
    for t in range(own):
        total = convolved_row(weights2, hidden[:, t * plane : (t + 1) * plane], fine_w, fine_d, outc)
        outs.append(jnp.maximum(total + bias2, 0.0).astype(jnp.bfloat16))
    out_ref[...] = rows_of(jnp.concatenate(outs, axis=0), outc, own, fine_d, fine_w)

    pl.when(me > 0)(upward.wait_send)
    pl.when(me < n - 1)(downward.wait_send)
    pltpu.make_async_copy(outgoing.at[pl.ds(0, n - 1)], incoming.at[pl.ds(0, n - 1)], coarse_send).wait()


def body(coarse, skip, up_weight, up_bias, conv1_weight, conv1_bias, conv2_weight, conv2_bias):
    n = lax.axis_size("ha")
    cup, depth, local_w, height = coarse.shape
    skipc, fine_d, own, fine_w = skip.shape
    outc = conv1_weight.shape[3]
    near = height // n
    width = local_w * n
    plane = fine_d * fine_w
    slab = -(-((near + 2) * depth * local_w) // ROW_TILE) * ROW_TILE
    need = (near + 2) * plane * (n * slab * 6 + 4 * 8 * cup) + (own + 4) * 27 * outc * plane * 4
    if need > VMEM_BUDGET or plane % 128 or near < 1 or own < MARGIN:
        return large_body(
            coarse, skip, up_weight, up_bias, conv1_weight, conv1_bias, conv2_weight, conv2_bias
        )
    operands = (
        jnp.transpose(coarse, (1, 2, 3, 0)).reshape(depth * local_w * height, cup),
        skip.reshape(skipc * fine_d * own, fine_w),
        up_weight.reshape(8 * cup, cup),
        up_bias[None],
        conv1_weight.reshape(27 * outc, cup + skipc),
        conv1_bias[None],
        conv2_weight.reshape(27 * outc, outc),
        conv2_bias[None],
    )
    out = pl.pallas_call(
        functools.partial(kernel, n, depth, width, height, slab),
        out_shape=jax.ShapeDtypeStruct((outc * fine_d * own, fine_w), jnp.bfloat16),
        in_specs=[pl.BlockSpec(memory_space=pltpu.HBM)] * len(operands),
        out_specs=pl.BlockSpec(memory_space=pltpu.VMEM),
        scratch_shapes=[pltpu.VMEM(operand.shape, operand.dtype) for operand in operands]
        + [
            pltpu.VMEM((n, slab, cup), jnp.bfloat16),
            pltpu.VMEM((n, slab, cup), jnp.bfloat16),
            pltpu.VMEM((own * skipc, plane), jnp.bfloat16),
            pltpu.VMEM((2, MARGIN * skipc, plane), jnp.bfloat16),
            pltpu.VMEM((3 * (cup + skipc), (own + 2) * plane), jnp.bfloat16),
            pltpu.VMEM((3 * outc, own * plane), jnp.bfloat16),
            pltpu.SemaphoreType.DMA,
            pltpu.SemaphoreType.DMA,
            pltpu.SemaphoreType.DMA((2,)),
            pltpu.SemaphoreType.DMA((2,)),
            pltpu.SemaphoreType.DMA((len(operands),)),
        ],
        compiler_params=pltpu.CompilerParams(
            collective_id=0, has_side_effects=True, vmem_limit_bytes=VMEM_LIMIT
        ),
    )(*operands)
    return out.reshape(outc, fine_d, own, fine_w)


def solution(mesh):
    return jax.shard_map(
        body,
        mesh=mesh,
        in_specs=(
            P(None, "groups", "ha", None),
            P(None, "groups", "ha", None),
            P(),
            P(),
            P(),
            P(),
            P(),
            P(),
        ),
        out_specs=P(None, "groups", "ha", None),
        check_vma=False,
    )
```

```python
import functools

import jax
import jax.numpy as jnp
from jax import lax
from jax.experimental import pallas as pl
from jax.experimental.pallas import tpu as pltpu
from jax.sharding import PartitionSpec as P

VMEM_BUDGET = 40 * 1024 * 1024
VMEM_LIMIT = 48 * 1024 * 1024
MARGIN = 2
ROW_TILE = 16
UNROLL = 1


def with_halo(array, sides, width):
    for axis, dim in sides:
        count, length = (lax.axis_size(axis), array.shape[dim])
        up = [(i, (i + 1) % count) for i in range(count - 1)]
        down = [(j, i) for i, j in up]
        last = lax.slice_in_dim(array, length - width, length, axis=dim)
        first = lax.slice_in_dim(array, 0, width, axis=dim)
        before = lax.ppermute(last, axis, up)
        after = lax.ppermute(first, axis, down)
        array = jnp.concatenate([before, array, after], axis=dim)
    return array


def upsample(inputs, weight, bias):
    values = jnp.einsum("abcoi,idpq->odapbqc", weight, inputs, preferred_element_type=jnp.float32)
    channels = weight.shape[3]
    values = values.reshape(channels, 2 * inputs.shape[1], 2 * inputs.shape[2], 2 * inputs.shape[3])
    return (values + bias[:, None, None, None]).astype(jnp.bfloat16)


def convolve(inputs, weight, bias):
    result = lax.conv_general_dilated(
        inputs[None],
        weight,
        (1, 1, 1),
        ((1, 1), (0, 0), (1, 1)),
        dimension_numbers=("NCDHW", "DHWOI", "NCDHW"),
        preferred_element_type=jnp.float32,
    )[0]
    return jnp.maximum(result + bias[:, None, None, None], 0.0).astype(jnp.bfloat16)


def inside_rows(height_rows, margin_rows):
    row_index = (
        lax.axis_index("ha") * height_rows
        - margin_rows
        + jnp.arange(height_rows + 2 * margin_rows, dtype=jnp.int32)
    )
    return (row_index >= 0) & (row_index < lax.axis_size("ha") * height_rows)


def large_body(coarse, skip, up_weight, up_bias, conv1_weight, conv1_bias, conv2_weight, conv2_bias):
    margin_rows = 2
    height_rows = skip.shape[2]
    local_fine = upsample(coarse, jnp.transpose(up_weight, (0, 2, 1, 3, 4)), up_bias)
    moved = lax.all_to_all(local_fine, "ha", split_axis=3, concat_axis=2, tiled=True)
    joined = jnp.concatenate([jnp.swapaxes(moved, 2, 3), skip], axis=0)
    padded = with_halo(joined, (("ha", 2),), margin_rows)
    widened = convolve(padded, conv1_weight, conv1_bias)
    inside = inside_rows(height_rows, 1)
    padded_hidden = jnp.where(inside[None, None, :, None], widened, jnp.zeros((), jnp.bfloat16))
    return convolve(padded_hidden, conv2_weight, conv2_bias)


def iota(shape, dim):
    return lax.broadcasted_iota(jnp.int32, shape, dim)


def column(row):
    size = row.shape[1]
    same = iota((size, size), 0) == iota((size, size), 1)
    return jnp.sum(jnp.where(same, row, 0.0), axis=1, keepdims=True)


def as_bits(mask):
    return jnp.where(mask, 1.0, 0.0).astype(jnp.bfloat16)


def one_hot(wanted, count):
    return as_bits(iota((wanted.shape[0], count), 1) == wanted)


def nt_dot(a, b):
    return lax.dot_general(a, b, (((1,), (1,)), ((), ())), preferred_element_type=jnp.float32)


def nn_dot(a, b):
    return lax.dot_general(a, b, (((1,), (0,)), ((), ())), preferred_element_type=jnp.float32)


def same_depth(channels, own, fine_d, fine_w):
    row = iota((channels * fine_d * own, 1), 0)
    lane = iota((1, fine_d * fine_w), 1)
    return lax.rem(lax.div(row, own), fine_d) == lax.div(lane, fine_w)


def width_tiles(fine_d, fine_w):
    shape = (fine_w, fine_d * fine_w)
    return as_bits(lax.rem(iota(shape, 1), fine_w) == iota(shape, 0))


def planes_of(rows, channels, own, fine_d, fine_w):
    wide = nn_dot(rows, width_tiles(fine_d, fine_w))
    wide = jnp.where(same_depth(channels, own, fine_d, fine_w), wide, 0.0).astype(jnp.bfloat16)
    at = iota((1, rows.shape[0]), 1)
    goal = lax.rem(at, own) * channels + lax.div(at, own * fine_d)
    return nn_dot(as_bits(iota((own * channels, 1), 0) == goal), wide).astype(jnp.bfloat16)


def stack_taps(weights, pieces, lanes):
    return jnp.concatenate([weights[at : at + size, lanes] for at, size in pieces], axis=1)


def moved_sum(taps, fine_w, fine_d, outc):
    plane = fine_w * fine_d
    lane = iota((1, plane), 1)
    x, z = lax.rem(lane, fine_w), lax.div(lane, fine_w)
    planes = []
    for p in range(3):
        before, here, after = (taps[(p * 3 + r) * outc : (p * 3 + r + 1) * outc] for r in range(3))
        here = here + jnp.where(x > 0, pltpu.roll(before, 1, 1), 0.0)
        here = here + jnp.where(x < fine_w - 1, pltpu.roll(after, plane - 1, 1), 0.0)
        planes.append(here)
    total = planes[1]
    total = total + jnp.where(z > 0, pltpu.roll(planes[0], fine_w, 1), 0.0)
    return total + jnp.where(z < fine_d - 1, pltpu.roll(planes[2], plane - fine_w, 1), 0.0)


def rows_at(ref, index, size, count=None):
    return ref.at[pl.ds(pl.multiple_of(index * size, size), size if count is None else count)]


def kernel(
    n, depth, width, height, slab,
    coarse_hbm, skip_hbm, upw_hbm, upb_hbm, w1_hbm, b1_hbm, w2_hbm, b2_hbm,
    out_ref,
    coarse_ref, skip_ref, upw_ref, upb_ref, w1_ref, b1_ref, w2_ref, b2_ref,
    outgoing, incoming, up_planes, skip_planes, hidden, outs, source, order, up_stack, up1, skip1, stack2, partial,
    coarse_send, coarse_recv, skip_send, skip_recv, load_sem,
):
    me = lax.axis_index("ha")
    cup, outc = upw_ref.shape[1], w2_ref.shape[1]
    skipc = w1_ref.shape[1] - cup
    near = height // n
    own = 2 * near
    local_w = width // n
    fine_w, fine_d = 2 * width, 2 * depth
    plane = fine_w * fine_d
    reach = own + 2 * MARGIN

    operands = (
        (coarse_hbm, coarse_ref), (skip_hbm, skip_ref), (w1_hbm, w1_ref), (w2_hbm, w2_ref),
        (upw_hbm, upw_ref), (upb_hbm, upb_ref), (b1_hbm, b1_ref), (b2_hbm, b2_ref),
    )
    loads = [pltpu.make_async_copy(src, dst, load_sem.at[i]) for i, (src, dst) in enumerate(operands)]
    for load in loads[:2]:
        load.start()
    barrier = pltpu.get_barrier_semaphore()
    for k in range(1, n):
        pl.semaphore_signal(
            barrier, inc=1, device_id={"ha": lax.rem(me + k, n)}, device_id_type=pl.DeviceIdType.MESH
        )
    for load in loads[2:]:
        load.start()

    at = iota((n * slab, 1), 0)
    to, slot = lax.div(at, slab), lax.rem(at, slab)
    row = to * near - 1 + lax.div(slot, depth * local_w)
    wanted = (lax.rem(lax.div(slot, local_w), depth) * local_w + lax.rem(slot, local_w)) * height + row
    real = (row >= 0) & (row < height) & (slot < (near + 2) * depth * local_w)
    pick = one_hot(jnp.where(real, wanted, -1), depth * local_w * height)
    loads[0].wait()
    outgoing[...] = nn_dot(pick, coarse_ref[...]).astype(jnp.bfloat16).reshape(n, slab, cup)
    pl.semaphore_wait(barrier, n - 1)

    for k in range(1, n):
        to = lax.rem(me + (n // 2 + k - 1) % (n - 1) + 1, n)
        pltpu.make_async_remote_copy(
            src_ref=outgoing.at[to], dst_ref=incoming.at[me],
            send_sem=coarse_send, recv_sem=coarse_recv,
            device_id={"ha": to}, device_id_type=pl.DeviceIdType.MESH,
        ).start()
    pltpu.make_async_copy(outgoing.at[me], incoming.at[me], coarse_recv).start()

    edge = MARGIN * skipc
    loads[1].wait()
    skip_planes[edge : edge + own * skipc] = planes_of(skip_ref[...], skipc, own, fine_d, fine_w)
    upward = pltpu.make_async_remote_copy(
        src_ref=skip_planes.at[pl.ds(edge, edge)], dst_ref=skip_planes.at[pl.ds((MARGIN + own) * skipc, edge)],
        send_sem=skip_send.at[0], recv_sem=skip_recv.at[0],
        device_id={"ha": jnp.maximum(me - 1, 0)}, device_id_type=pl.DeviceIdType.MESH,
    )
    downward = pltpu.make_async_remote_copy(
        src_ref=skip_planes.at[pl.ds(own * skipc, edge)], dst_ref=skip_planes.at[pl.ds(0, edge)],
        send_sem=skip_send.at[1], recv_sem=skip_recv.at[1],
        device_id={"ha": jnp.minimum(me + 1, n - 1)}, device_id_type=pl.DeviceIdType.MESH,
    )
    pl.when(me > 0)(upward.start)
    pl.when(me < n - 1)(downward.start)

    @pl.when(me == 0)
    def _():
        skip_planes[:edge] = jnp.zeros((edge, plane), skip_planes.dtype)

    @pl.when(me == n - 1)
    def _():
        skip_planes[(MARGIN + own) * skipc :] = jnp.zeros((edge, plane), skip_planes.dtype)

    at = iota((plane, 1), 0)
    z, x = lax.div(at, fine_w), lax.rem(at, fine_w)
    w = lax.div(x, 2)
    taken = lax.div(w, local_w) * slab + lax.div(z, 2) * local_w + lax.rem(w, local_w)
    parity = lax.rem(z, 2) * 2 + lax.rem(x, 2)

    def fill_source(h, _):
        rows_at(source, h, plane)[...] = one_hot(taken + h * (depth * local_w), n * slab)

    lax.fori_loop(0, near + 2, fill_source, None)

    chunk = fine_d * own

    def fill_order(o, _):
        rows_at(order, o, chunk)[...] = one_hot(iota((chunk, 1), 0) * outc + o, chunk * outc)

    lax.fori_loop(0, outc, fill_order, None)

    for load in loads[2:]:
        load.wait()
    for b in range(2):
        pieces = [(((a * 2 + b) * 2 + c) * cup, cup) for a in range(2) for c in range(2)]
        up_stack[b * cup : (b + 1) * cup] = stack_taps(upw_ref, pieces, slice(None))
    block = 3 * outc
    for p in range(3):
        pieces = [((p * 3 + q) * block, block) for q in range(3)]
        rows = slice(p * block, (p + 1) * block)
        up1[rows] = stack_taps(w1_ref, pieces, slice(0, cup))
        skip1[rows] = stack_taps(w1_ref, pieces, slice(cup, cup + skipc))
        stack2[rows] = stack_taps(w2_ref, pieces, slice(None))
    up_bias, bias1, bias2 = column(upb_ref[...]), column(b1_ref[...]), column(b2_ref[...])
    up_bias = jnp.concatenate([up_bias, up_bias], axis=0)

    def inside(row):
        return (me * own + row >= 0) & (me * own + row < n * own)

    pl.when(me < n - 1)(upward.wait_recv)
    pl.when(me > 0)(downward.wait_recv)

    def convolve_skip(t, _):
        rows_at(partial, t, 9 * outc)[...] = nn_dot(skip1[...], rows_at(skip_planes, t, skipc, 3 * skipc)[...])

    lax.fori_loop(0, own + 2, convolve_skip, None)
    pltpu.make_async_copy(incoming, incoming, coarse_recv).wait()

    received = incoming[...].reshape(n * slab, cup)
    received = jnp.concatenate([received] * 4, axis=1)
    mine = parity == lax.div(iota((1, 4 * cup), 1), cup)

    def upsample_row(h, _):
        spread = nn_dot(rows_at(source, h, plane)[...], received)
        spread = jnp.where(mine, spread, 0.0).astype(jnp.bfloat16)
        values = nt_dot(up_stack[...], spread) + up_bias
        values = jnp.where(inside(2 * h - MARGIN), values, 0.0)
        rows_at(up_planes, h, 2 * cup)[...] = values.astype(jnp.bfloat16)

    lax.fori_loop(0, near + 2, upsample_row, None, unroll=UNROLL)

    def convolve_joined(t, _):
        taps = nn_dot(up1[...], rows_at(up_planes, t, cup, 3 * cup)[...]) + rows_at(partial, t, 9 * outc)[...]
        values = jnp.maximum(moved_sum(taps, fine_w, fine_d, outc) + bias1, 0.0)
        values = jnp.where(inside(t - 1), values, 0.0)
        rows_at(hidden, t, outc)[...] = values.astype(jnp.bfloat16)

    lax.fori_loop(0, own + 2, convolve_joined, None, unroll=UNROLL)

    def convolve_hidden(t, _):
        taps = nn_dot(stack2[...], rows_at(hidden, t, outc, 3 * outc)[...])
        values = jnp.maximum(moved_sum(taps, fine_w, fine_d, outc) + bias2, 0.0)
        rows_at(outs, t, outc)[...] = values.astype(jnp.bfloat16)

    lax.fori_loop(0, own, convolve_hidden, None, unroll=UNROLL)
    slices = [outs[:, z * fine_w : (z + 1) * fine_w] for z in range(fine_d)]
    out_ref[...] = nn_dot(order[...], jnp.concatenate(slices, axis=0)).astype(jnp.bfloat16)

    pl.when(me > 0)(upward.wait_send)
    pl.when(me < n - 1)(downward.wait_send)
    pltpu.make_async_copy(outgoing.at[pl.ds(0, n - 1)], incoming.at[pl.ds(0, n - 1)], coarse_send).wait()


def body(coarse, skip, up_weight, up_bias, conv1_weight, conv1_bias, conv2_weight, conv2_bias):
    n = lax.axis_size("ha")
    cup, depth, local_w, height = coarse.shape
    skipc, fine_d, own, fine_w = skip.shape
    outc = conv1_weight.shape[3]
    near = height // n
    width = local_w * n
    plane = fine_d * fine_w
    slab = -(-((near + 2) * depth * local_w) // ROW_TILE) * ROW_TILE
    need = (near + 2) * plane * (n * slab * 6 + 4 * 8 * cup) + (own + 4) * 27 * outc * plane * 4
    if need > VMEM_BUDGET or plane % 128 or near < 1 or own < MARGIN:
        return large_body(
            coarse, skip, up_weight, up_bias, conv1_weight, conv1_bias, conv2_weight, conv2_bias
        )
    reach = own + 2 * MARGIN
    operands = (
        jnp.transpose(coarse, (1, 2, 3, 0)).reshape(depth * local_w * height, cup),
        skip.reshape(skipc * fine_d * own, fine_w),
        up_weight.reshape(8 * cup, cup),
        up_bias[None],
        conv1_weight.reshape(27 * outc, cup + skipc),
        conv1_bias[None],
        conv2_weight.reshape(27 * outc, outc),
        conv2_bias[None],
    )
    out = pl.pallas_call(
        functools.partial(kernel, n, depth, width, height, slab),
        out_shape=pltpu.VMEM((outc * fine_d * own, fine_w), jnp.bfloat16),
        in_specs=[pl.BlockSpec(memory_space=pltpu.HBM)] * len(operands),
        out_specs=pl.BlockSpec(memory_space=pltpu.VMEM),
        scratch_shapes=[pltpu.VMEM(operand.shape, operand.dtype) for operand in operands]
        + [
            pltpu.VMEM((n, slab, cup), jnp.bfloat16),
            pltpu.VMEM((n, slab, cup), jnp.bfloat16),
            pltpu.VMEM((reach * cup, plane), jnp.bfloat16),
            pltpu.VMEM((reach * skipc, plane), jnp.bfloat16),
            pltpu.VMEM(((own + 2) * outc, plane), jnp.bfloat16),
            pltpu.VMEM((own * outc, plane), jnp.bfloat16),
            pltpu.VMEM(((near + 2) * plane, n * slab), jnp.bfloat16),
            pltpu.VMEM((outc * fine_d * own, outc * fine_d * own), jnp.bfloat16),
            pltpu.VMEM((2 * cup, 4 * cup), jnp.bfloat16),
            pltpu.VMEM((9 * outc, 3 * cup), jnp.bfloat16),
            pltpu.VMEM((9 * outc, 3 * skipc), jnp.bfloat16),
            pltpu.VMEM((9 * outc, 3 * outc), jnp.bfloat16),
            pltpu.VMEM(((own + 2) * 9 * outc, plane), jnp.float32),
            pltpu.SemaphoreType.DMA,
            pltpu.SemaphoreType.DMA,
            pltpu.SemaphoreType.DMA((2,)),
            pltpu.SemaphoreType.DMA((2,)),
            pltpu.SemaphoreType.DMA((len(operands),)),
        ],
        compiler_params=pltpu.CompilerParams(
            collective_id=0, has_side_effects=True, vmem_limit_bytes=VMEM_LIMIT
        ),
    )(*(pltpu.with_memory_space_constraint(operand, pltpu.HBM) for operand in operands))
    return out.reshape(outc, fine_d, own, fine_w)


def solution(mesh):
    return jax.shard_map(
        body,
        mesh=mesh,
        in_specs=(
            P(None, "groups", "ha", None),
            P(None, "groups", "ha", None),
            P(),
            P(),
            P(),
            P(),
            P(),
            P(),
        ),
        out_specs=P(None, "groups", "ha", None),
        check_vma=False,
    )
```

```python
import functools

import jax
import jax.numpy as jnp
from jax import lax
from jax.experimental import pallas as pl
from jax.experimental.pallas import tpu as pltpu
from jax.sharding import PartitionSpec as P

VMEM_BUDGET = 40 * 1024 * 1024
VMEM_LIMIT = 48 * 1024 * 1024
MARGIN = 2
ROW_TILE = 16


def with_halo(array, sides, width):
    for axis, dim in sides:
        count, length = (lax.axis_size(axis), array.shape[dim])
        up = [(i, (i + 1) % count) for i in range(count - 1)]
        down = [(j, i) for i, j in up]
        last = lax.slice_in_dim(array, length - width, length, axis=dim)
        first = lax.slice_in_dim(array, 0, width, axis=dim)
        before = lax.ppermute(last, axis, up)
        after = lax.ppermute(first, axis, down)
        array = jnp.concatenate([before, array, after], axis=dim)
    return array


def upsample(inputs, weight, bias):
    values = jnp.einsum("abcoi,idpq->odapbqc", weight, inputs, preferred_element_type=jnp.float32)
    channels = weight.shape[3]
    values = values.reshape(channels, 2 * inputs.shape[1], 2 * inputs.shape[2], 2 * inputs.shape[3])
    return (values + bias[:, None, None, None]).astype(jnp.bfloat16)


def convolve(inputs, weight, bias):
    result = lax.conv_general_dilated(
        inputs[None],
        weight,
        (1, 1, 1),
        ((1, 1), (0, 0), (1, 1)),
        dimension_numbers=("NCDHW", "DHWOI", "NCDHW"),
        preferred_element_type=jnp.float32,
    )[0]
    return jnp.maximum(result + bias[:, None, None, None], 0.0).astype(jnp.bfloat16)


def inside_rows(height_rows, margin_rows):
    row_index = (
        lax.axis_index("ha") * height_rows
        - margin_rows
        + jnp.arange(height_rows + 2 * margin_rows, dtype=jnp.int32)
    )
    return (row_index >= 0) & (row_index < lax.axis_size("ha") * height_rows)


def large_body(coarse, skip, up_weight, up_bias, conv1_weight, conv1_bias, conv2_weight, conv2_bias):
    margin_rows = 2
    height_rows = skip.shape[2]
    local_fine = upsample(coarse, jnp.transpose(up_weight, (0, 2, 1, 3, 4)), up_bias)
    moved = lax.all_to_all(local_fine, "ha", split_axis=3, concat_axis=2, tiled=True)
    joined = jnp.concatenate([jnp.swapaxes(moved, 2, 3), skip], axis=0)
    padded = with_halo(joined, (("ha", 2),), margin_rows)
    widened = convolve(padded, conv1_weight, conv1_bias)
    inside = inside_rows(height_rows, 1)
    padded_hidden = jnp.where(inside[None, None, :, None], widened, jnp.zeros((), jnp.bfloat16))
    return convolve(padded_hidden, conv2_weight, conv2_bias)


def iota(shape, dim):
    return lax.broadcasted_iota(jnp.int32, shape, dim)


def column(row):
    size = row.shape[1]
    same = iota((size, size), 0) == iota((size, size), 1)
    return jnp.sum(jnp.where(same, row, 0.0), axis=1, keepdims=True)


def as_bits(mask):
    return jnp.where(mask, 1.0, 0.0).astype(jnp.bfloat16)


def one_hot(wanted, count):
    return as_bits(iota((wanted.shape[0], count), 1) == wanted)


def nt_dot(a, b):
    return lax.dot_general(a, b, (((1,), (1,)), ((), ())), preferred_element_type=jnp.float32)


def nn_dot(a, b):
    return lax.dot_general(a, b, (((1,), (0,)), ((), ())), preferred_element_type=jnp.float32)


def same_depth(channels, own, fine_d, fine_w):
    row = iota((channels * fine_d * own, 1), 0)
    lane = iota((1, fine_d * fine_w), 1)
    return lax.rem(lax.div(row, own), fine_d) == lax.div(lane, fine_w)


def width_tiles(fine_d, fine_w):
    shape = (fine_w, fine_d * fine_w)
    return as_bits(lax.rem(iota(shape, 1), fine_w) == iota(shape, 0))


def planes_of(rows, channels, own, fine_d, fine_w):
    wide = nn_dot(rows, width_tiles(fine_d, fine_w))
    wide = jnp.where(same_depth(channels, own, fine_d, fine_w), wide, 0.0).astype(jnp.bfloat16)
    at = iota((1, rows.shape[0]), 1)
    goal = lax.rem(at, own) * channels + lax.div(at, own * fine_d)
    return nn_dot(as_bits(iota((own * channels, 1), 0) == goal), wide).astype(jnp.bfloat16)


def stack_taps(weights, pieces, lanes):
    return jnp.concatenate([weights[at : at + size, lanes] for at, size in pieces], axis=1)


def moved_sum(taps, fine_w, fine_d, outc):
    plane = fine_w * fine_d
    lane = iota((1, plane), 1)
    x, z = lax.rem(lane, fine_w), lax.div(lane, fine_w)
    planes = []
    for p in range(3):
        before, here, after = (taps[(p * 3 + r) * outc : (p * 3 + r + 1) * outc] for r in range(3))
        here = here + jnp.where(x > 0, pltpu.roll(before, 1, 1), 0.0)
        here = here + jnp.where(x < fine_w - 1, pltpu.roll(after, plane - 1, 1), 0.0)
        planes.append(here)
    total = planes[1]
    total = total + jnp.where(z > 0, pltpu.roll(planes[0], fine_w, 1), 0.0)
    return total + jnp.where(z < fine_d - 1, pltpu.roll(planes[2], plane - fine_w, 1), 0.0)


def rows_at(ref, index, size, count=None):
    first = index * size if isinstance(index, int) else pl.multiple_of(index * size, size)
    return ref.at[pl.ds(first, size if count is None else count)]


def kernel(
    n, depth, width, height, slab,
    coarse_hbm, skip_hbm, upw_hbm, upb_hbm, w1_hbm, b1_hbm, w2_hbm, b2_hbm,
    out_ref,
    coarse_ref, skip_ref, upw_ref, upb_ref, w1_ref, b1_ref, w2_ref, b2_ref,
    outgoing, incoming, up_planes, skip_planes, hidden, outs, source, order, up_stack, up1, skip1, stack2, partial,
    coarse_send, coarse_recv, skip_send, skip_recv, load_sem,
):
    me = lax.axis_index("ha")
    cup, outc = upw_ref.shape[1], w2_ref.shape[1]
    skipc = w1_ref.shape[1] - cup
    near = height // n
    own = 2 * near
    local_w = width // n
    fine_w, fine_d = 2 * width, 2 * depth
    plane = fine_w * fine_d
    reach = own + 2 * MARGIN

    operands = (
        (coarse_hbm, coarse_ref), (skip_hbm, skip_ref), (w1_hbm, w1_ref), (w2_hbm, w2_ref),
        (upw_hbm, upw_ref), (upb_hbm, upb_ref), (b1_hbm, b1_ref), (b2_hbm, b2_ref),
    )
    loads = [pltpu.make_async_copy(src, dst, load_sem.at[i]) for i, (src, dst) in enumerate(operands)]
    for load in loads[:2]:
        load.start()
    barrier = pltpu.get_barrier_semaphore()
    for k in range(1, n):
        pl.semaphore_signal(
            barrier, inc=1, device_id={"ha": lax.rem(me + k, n)}, device_id_type=pl.DeviceIdType.MESH
        )
    for load in loads[2:]:
        load.start()

    at = iota((n * slab, 1), 0)
    to, slot = lax.div(at, slab), lax.rem(at, slab)
    row = to * near - 1 + lax.div(slot, depth * local_w)
    wanted = (lax.rem(lax.div(slot, local_w), depth) * local_w + lax.rem(slot, local_w)) * height + row
    real = (row >= 0) & (row < height) & (slot < (near + 2) * depth * local_w)
    pick = one_hot(jnp.where(real, wanted, -1), depth * local_w * height)
    loads[0].wait()
    outgoing[...] = nn_dot(pick, coarse_ref[...]).astype(jnp.bfloat16).reshape(n, slab, cup)
    pl.semaphore_wait(barrier, n - 1)

    for k in range(1, n):
        to = lax.rem(me + (n // 2 + k - 1) % (n - 1) + 1, n)
        pltpu.make_async_remote_copy(
            src_ref=outgoing.at[to], dst_ref=incoming.at[me],
            send_sem=coarse_send, recv_sem=coarse_recv,
            device_id={"ha": to}, device_id_type=pl.DeviceIdType.MESH,
        ).start()
    pltpu.make_async_copy(outgoing.at[me], incoming.at[me], coarse_recv).start()

    edge = MARGIN * skipc
    loads[1].wait()
    skip_planes[edge : edge + own * skipc] = planes_of(skip_ref[...], skipc, own, fine_d, fine_w)
    upward = pltpu.make_async_remote_copy(
        src_ref=skip_planes.at[pl.ds(edge, edge)], dst_ref=skip_planes.at[pl.ds((MARGIN + own) * skipc, edge)],
        send_sem=skip_send.at[0], recv_sem=skip_recv.at[0],
        device_id={"ha": jnp.maximum(me - 1, 0)}, device_id_type=pl.DeviceIdType.MESH,
    )
    downward = pltpu.make_async_remote_copy(
        src_ref=skip_planes.at[pl.ds(own * skipc, edge)], dst_ref=skip_planes.at[pl.ds(0, edge)],
        send_sem=skip_send.at[1], recv_sem=skip_recv.at[1],
        device_id={"ha": jnp.minimum(me + 1, n - 1)}, device_id_type=pl.DeviceIdType.MESH,
    )
    pl.when(me > 0)(upward.start)
    pl.when(me < n - 1)(downward.start)

    @pl.when(me == 0)
    def _():
        skip_planes[:edge] = jnp.zeros((edge, plane), skip_planes.dtype)

    @pl.when(me == n - 1)
    def _():
        skip_planes[(MARGIN + own) * skipc :] = jnp.zeros((edge, plane), skip_planes.dtype)

    at = iota((plane, 1), 0)
    z, x = lax.div(at, fine_w), lax.rem(at, fine_w)
    w = lax.div(x, 2)
    taken = lax.div(w, local_w) * slab + lax.div(z, 2) * local_w + lax.rem(w, local_w)
    parity = lax.rem(z, 2) * 2 + lax.rem(x, 2)

    def fill_source(h, _):
        rows_at(source, h, plane)[...] = one_hot(taken + h * (depth * local_w), n * slab)

    for i in range(near + 2):
        fill_source(i, None)

    chunk = fine_d * own

    def fill_order(o, _):
        rows_at(order, o, chunk)[...] = one_hot(iota((chunk, 1), 0) * outc + o, chunk * outc)

    lax.fori_loop(0, outc, fill_order, None)

    for load in loads[2:]:
        load.wait()
    for b in range(2):
        pieces = [(((a * 2 + b) * 2 + c) * cup, cup) for a in range(2) for c in range(2)]
        up_stack[b * cup : (b + 1) * cup] = stack_taps(upw_ref, pieces, slice(None))
    block = 3 * outc
    for p in range(3):
        pieces = [((p * 3 + q) * block, block) for q in range(3)]
        rows = slice(p * block, (p + 1) * block)
        up1[rows] = stack_taps(w1_ref, pieces, slice(0, cup))
        skip1[rows] = stack_taps(w1_ref, pieces, slice(cup, cup + skipc))
        stack2[rows] = stack_taps(w2_ref, pieces, slice(None))
    up_bias, bias1, bias2 = column(upb_ref[...]), column(b1_ref[...]), column(b2_ref[...])
    up_bias = jnp.concatenate([up_bias, up_bias], axis=0)

    def inside(row):
        return (me * own + row >= 0) & (me * own + row < n * own)

    pl.when(me < n - 1)(upward.wait_recv)
    pl.when(me > 0)(downward.wait_recv)

    def convolve_skip(t, _):
        rows_at(partial, t, 9 * outc)[...] = nn_dot(skip1[...], rows_at(skip_planes, t, skipc, 3 * skipc)[...])

    for i in range(own + 2):
        convolve_skip(i, None)
    pltpu.make_async_copy(incoming, incoming, coarse_recv).wait()

    received = incoming[...].reshape(n * slab, cup)
    received = jnp.concatenate([received] * 4, axis=1)
    mine = parity == lax.div(iota((1, 4 * cup), 1), cup)

    def upsample_row(h, _):
        spread = nn_dot(rows_at(source, h, plane)[...], received)
        spread = jnp.where(mine, spread, 0.0).astype(jnp.bfloat16)
        values = nt_dot(up_stack[...], spread) + up_bias
        values = jnp.where(inside(2 * h - MARGIN), values, 0.0)
        rows_at(up_planes, h, 2 * cup)[...] = values.astype(jnp.bfloat16)

    for i in range(near + 2):
        upsample_row(i, None)

    def convolve_joined(t, _):
        taps = nn_dot(up1[...], rows_at(up_planes, t, cup, 3 * cup)[...]) + rows_at(partial, t, 9 * outc)[...]
        values = jnp.maximum(moved_sum(taps, fine_w, fine_d, outc) + bias1, 0.0)
        values = jnp.where(inside(t - 1), values, 0.0)
        rows_at(hidden, t, outc)[...] = values.astype(jnp.bfloat16)

    for i in range(own + 2):
        convolve_joined(i, None)

    def convolve_hidden(t, _):
        taps = nn_dot(stack2[...], rows_at(hidden, t, outc, 3 * outc)[...])
        values = jnp.maximum(moved_sum(taps, fine_w, fine_d, outc) + bias2, 0.0)
        rows_at(outs, t, outc)[...] = values.astype(jnp.bfloat16)

    for i in range(own):
        convolve_hidden(i, None)
    slices = [outs[:, z * fine_w : (z + 1) * fine_w] for z in range(fine_d)]
    out_ref[...] = nn_dot(order[...], jnp.concatenate(slices, axis=0)).astype(jnp.bfloat16)

    pl.when(me > 0)(upward.wait_send)
    pl.when(me < n - 1)(downward.wait_send)
    pltpu.make_async_copy(outgoing.at[pl.ds(0, n - 1)], incoming.at[pl.ds(0, n - 1)], coarse_send).wait()


def body(coarse, skip, up_weight, up_bias, conv1_weight, conv1_bias, conv2_weight, conv2_bias):
    n = lax.axis_size("ha")
    cup, depth, local_w, height = coarse.shape
    skipc, fine_d, own, fine_w = skip.shape
    outc = conv1_weight.shape[3]
    near = height // n
    width = local_w * n
    plane = fine_d * fine_w
    slab = -(-((near + 2) * depth * local_w) // ROW_TILE) * ROW_TILE
    need = (near + 2) * plane * (n * slab * 6 + 4 * 8 * cup) + (own + 4) * 27 * outc * plane * 4
    if need > VMEM_BUDGET or plane % 128 or near < 1 or own < MARGIN:
        return large_body(
            coarse, skip, up_weight, up_bias, conv1_weight, conv1_bias, conv2_weight, conv2_bias
        )
    reach = own + 2 * MARGIN
    operands = (
        jnp.transpose(coarse, (1, 2, 3, 0)).reshape(depth * local_w * height, cup),
        skip.reshape(skipc * fine_d * own, fine_w),
        up_weight.reshape(8 * cup, cup),
        up_bias[None],
        conv1_weight.reshape(27 * outc, cup + skipc),
        conv1_bias[None],
        conv2_weight.reshape(27 * outc, outc),
        conv2_bias[None],
    )
    out = pl.pallas_call(
        functools.partial(kernel, n, depth, width, height, slab),
        out_shape=pltpu.VMEM((outc * fine_d * own, fine_w), jnp.bfloat16),
        in_specs=[pl.BlockSpec(memory_space=pltpu.HBM)] * len(operands),
        out_specs=pl.BlockSpec(memory_space=pltpu.VMEM),
        scratch_shapes=[pltpu.VMEM(operand.shape, operand.dtype) for operand in operands]
        + [
            pltpu.VMEM((n, slab, cup), jnp.bfloat16),
            pltpu.VMEM((n, slab, cup), jnp.bfloat16),
            pltpu.VMEM((reach * cup, plane), jnp.bfloat16),
            pltpu.VMEM((reach * skipc, plane), jnp.bfloat16),
            pltpu.VMEM(((own + 2) * outc, plane), jnp.bfloat16),
            pltpu.VMEM((own * outc, plane), jnp.bfloat16),
            pltpu.VMEM(((near + 2) * plane, n * slab), jnp.bfloat16),
            pltpu.VMEM((outc * fine_d * own, outc * fine_d * own), jnp.bfloat16),
            pltpu.VMEM((2 * cup, 4 * cup), jnp.bfloat16),
            pltpu.VMEM((9 * outc, 3 * cup), jnp.bfloat16),
            pltpu.VMEM((9 * outc, 3 * skipc), jnp.bfloat16),
            pltpu.VMEM((9 * outc, 3 * outc), jnp.bfloat16),
            pltpu.VMEM(((own + 2) * 9 * outc, plane), jnp.float32),
            pltpu.SemaphoreType.DMA,
            pltpu.SemaphoreType.DMA,
            pltpu.SemaphoreType.DMA((2,)),
            pltpu.SemaphoreType.DMA((2,)),
            pltpu.SemaphoreType.DMA((len(operands),)),
        ],
        compiler_params=pltpu.CompilerParams(
            collective_id=0, has_side_effects=True, vmem_limit_bytes=VMEM_LIMIT
        ),
    )(*(pltpu.with_memory_space_constraint(operand, pltpu.HBM) for operand in operands))
    return out.reshape(outc, fine_d, own, fine_w)


def solution(mesh):
    return jax.shard_map(
        body,
        mesh=mesh,
        in_specs=(
            P(None, "groups", "ha", None),
            P(None, "groups", "ha", None),
            P(),
            P(),
            P(),
            P(),
            P(),
            P(),
        ),
        out_specs=P(None, "groups", "ha", None),
        check_vma=False,
    )
```

```python
import functools

import jax
import jax.numpy as jnp
from jax import lax
from jax.experimental import pallas as pl
from jax.experimental.pallas import tpu as pltpu
from jax.sharding import PartitionSpec as P

VMEM_BUDGET = 40 * 1024 * 1024
VMEM_LIMIT = 48 * 1024 * 1024
MARGIN = 2
ROW_TILE = 16


def with_halo(array, sides, width):
    for axis, dim in sides:
        count, length = (lax.axis_size(axis), array.shape[dim])
        up = [(i, (i + 1) % count) for i in range(count - 1)]
        down = [(j, i) for i, j in up]
        last = lax.slice_in_dim(array, length - width, length, axis=dim)
        first = lax.slice_in_dim(array, 0, width, axis=dim)
        before = lax.ppermute(last, axis, up)
        after = lax.ppermute(first, axis, down)
        array = jnp.concatenate([before, array, after], axis=dim)
    return array


def upsample(inputs, weight, bias):
    values = jnp.einsum("abcoi,idpq->odapbqc", weight, inputs, preferred_element_type=jnp.float32)
    channels = weight.shape[3]
    values = values.reshape(channels, 2 * inputs.shape[1], 2 * inputs.shape[2], 2 * inputs.shape[3])
    return (values + bias[:, None, None, None]).astype(jnp.bfloat16)


def convolve(inputs, weight, bias):
    result = lax.conv_general_dilated(
        inputs[None],
        weight,
        (1, 1, 1),
        ((1, 1), (0, 0), (1, 1)),
        dimension_numbers=("NCDHW", "DHWOI", "NCDHW"),
        preferred_element_type=jnp.float32,
    )[0]
    return jnp.maximum(result + bias[:, None, None, None], 0.0).astype(jnp.bfloat16)


def inside_rows(height_rows, margin_rows):
    row_index = (
        lax.axis_index("ha") * height_rows
        - margin_rows
        + jnp.arange(height_rows + 2 * margin_rows, dtype=jnp.int32)
    )
    return (row_index >= 0) & (row_index < lax.axis_size("ha") * height_rows)


def large_body(coarse, skip, up_weight, up_bias, conv1_weight, conv1_bias, conv2_weight, conv2_bias):
    margin_rows = 2
    height_rows = skip.shape[2]
    local_fine = upsample(coarse, jnp.transpose(up_weight, (0, 2, 1, 3, 4)), up_bias)
    moved = lax.all_to_all(local_fine, "ha", split_axis=3, concat_axis=2, tiled=True)
    joined = jnp.concatenate([jnp.swapaxes(moved, 2, 3), skip], axis=0)
    padded = with_halo(joined, (("ha", 2),), margin_rows)
    widened = convolve(padded, conv1_weight, conv1_bias)
    inside = inside_rows(height_rows, 1)
    padded_hidden = jnp.where(inside[None, None, :, None], widened, jnp.zeros((), jnp.bfloat16))
    return convolve(padded_hidden, conv2_weight, conv2_bias)


def iota(shape, dim):
    return lax.broadcasted_iota(jnp.int32, shape, dim)


def column(row):
    size = row.shape[1]
    same = iota((size, size), 0) == iota((size, size), 1)
    return jnp.sum(jnp.where(same, row, 0.0), axis=1, keepdims=True)


def as_bits(mask):
    return jnp.where(mask, 1.0, 0.0).astype(jnp.bfloat16)


def one_hot(wanted, count):
    return as_bits(iota((wanted.shape[0], count), 1) == wanted)


def nt_dot(a, b):
    return lax.dot_general(a, b, (((1,), (1,)), ((), ())), preferred_element_type=jnp.float32)


def nn_dot(a, b):
    return lax.dot_general(a, b, (((1,), (0,)), ((), ())), preferred_element_type=jnp.float32)


def same_depth(channels, own, fine_d, fine_w):
    row = iota((channels * fine_d * own, 1), 0)
    lane = iota((1, fine_d * fine_w), 1)
    return lax.rem(lax.div(row, own), fine_d) == lax.div(lane, fine_w)


def width_tiles(fine_d, fine_w):
    shape = (fine_w, fine_d * fine_w)
    return as_bits(lax.rem(iota(shape, 1), fine_w) == iota(shape, 0))


def planes_of(rows, channels, own, fine_d, fine_w):
    wide = nn_dot(rows, width_tiles(fine_d, fine_w))
    wide = jnp.where(same_depth(channels, own, fine_d, fine_w), wide, 0.0).astype(jnp.bfloat16)
    at = iota((1, rows.shape[0]), 1)
    goal = lax.rem(at, own) * channels + lax.div(at, own * fine_d)
    return nn_dot(as_bits(iota((own * channels, 1), 0) == goal), wide).astype(jnp.bfloat16)


def stack_taps(weights, pieces, lanes):
    return jnp.concatenate([weights[at : at + size, lanes] for at, size in pieces], axis=1)


def moved_sum(taps, fine_w, fine_d, outc):
    plane = fine_w * fine_d
    lane = iota((1, plane), 1)
    x, z = lax.rem(lane, fine_w), lax.div(lane, fine_w)
    planes = []
    for p in range(3):
        before, here, after = (taps[(p * 3 + r) * outc : (p * 3 + r + 1) * outc] for r in range(3))
        here = here + jnp.where(x > 0, pltpu.roll(before, 1, 1), 0.0)
        here = here + jnp.where(x < fine_w - 1, pltpu.roll(after, plane - 1, 1), 0.0)
        planes.append(here)
    total = planes[1]
    total = total + jnp.where(z > 0, pltpu.roll(planes[0], fine_w, 1), 0.0)
    return total + jnp.where(z < fine_d - 1, pltpu.roll(planes[2], plane - fine_w, 1), 0.0)


def rows_at(ref, index, size, count=None):
    first = index * size if isinstance(index, int) else pl.multiple_of(index * size, size)
    return ref.at[pl.ds(first, size if count is None else count)]


def kernel(
    n, depth, width, height, slab,
    coarse_hbm, skip_hbm, upw_hbm, upb_hbm, w1_hbm, b1_hbm, w2_hbm, b2_hbm,
    out_ref,
    coarse_ref, skip_ref, upw_ref, upb_ref, w1_ref, b1_ref, w2_ref, b2_ref,
    outgoing, incoming, up_planes, skip_planes, hidden, outs, source, order, up_stack, up1, skip1, stack2, partial,
    coarse_send, coarse_recv, skip_send, skip_recv, load_sem,
):
    me = lax.axis_index("ha")
    cup, outc = upw_ref.shape[1], w2_ref.shape[1]
    skipc = w1_ref.shape[1] - cup
    near = height // n
    own = 2 * near
    local_w = width // n
    fine_w, fine_d = 2 * width, 2 * depth
    plane = fine_w * fine_d
    reach = own + 2 * MARGIN

    operands = (
        (coarse_hbm, coarse_ref), (skip_hbm, skip_ref), (w1_hbm, w1_ref), (w2_hbm, w2_ref),
        (upw_hbm, upw_ref), (upb_hbm, upb_ref), (b1_hbm, b1_ref), (b2_hbm, b2_ref),
    )
    loads = [pltpu.make_async_copy(src, dst, load_sem.at[i]) for i, (src, dst) in enumerate(operands)]
    for load in loads[:2]:
        load.start()
    barrier = pltpu.get_barrier_semaphore()
    for k in range(1, n):
        pl.semaphore_signal(
            barrier, inc=1, device_id={"ha": lax.rem(me + k, n)}, device_id_type=pl.DeviceIdType.MESH
        )
    for load in loads[2:]:
        load.start()

    at = iota((n * slab, 1), 0)
    to, slot = lax.div(at, slab), lax.rem(at, slab)
    row = to * near - 1 + lax.div(slot, depth * local_w)
    wanted = (lax.rem(lax.div(slot, local_w), depth) * local_w + lax.rem(slot, local_w)) * height + row
    real = (row >= 0) & (row < height) & (slot < (near + 2) * depth * local_w)
    pick = one_hot(jnp.where(real, wanted, -1), depth * local_w * height)
    loads[0].wait()
    twice = jnp.concatenate([coarse_ref[...]] * 2, axis=1)
    outgoing[...] = nn_dot(pick, twice).astype(jnp.bfloat16).reshape(n, slab, 2 * cup)
    pl.semaphore_wait(barrier, n - 1)

    for k in range(1, n):
        to = lax.rem(me + (n // 2 + k - 1) % (n - 1) + 1, n)
        pltpu.make_async_remote_copy(
            src_ref=outgoing.at[to], dst_ref=incoming.at[me],
            send_sem=coarse_send, recv_sem=coarse_recv,
            device_id={"ha": to}, device_id_type=pl.DeviceIdType.MESH,
        ).start()
    pltpu.make_async_copy(outgoing.at[me], incoming.at[me], coarse_recv).start()

    edge = MARGIN * skipc
    loads[1].wait()
    skip_planes[edge : edge + own * skipc] = planes_of(skip_ref[...], skipc, own, fine_d, fine_w)
    upward = pltpu.make_async_remote_copy(
        src_ref=skip_planes.at[pl.ds(edge, edge)], dst_ref=skip_planes.at[pl.ds((MARGIN + own) * skipc, edge)],
        send_sem=skip_send.at[0], recv_sem=skip_recv.at[0],
        device_id={"ha": jnp.maximum(me - 1, 0)}, device_id_type=pl.DeviceIdType.MESH,
    )
    downward = pltpu.make_async_remote_copy(
        src_ref=skip_planes.at[pl.ds(own * skipc, edge)], dst_ref=skip_planes.at[pl.ds(0, edge)],
        send_sem=skip_send.at[1], recv_sem=skip_recv.at[1],
        device_id={"ha": jnp.minimum(me + 1, n - 1)}, device_id_type=pl.DeviceIdType.MESH,
    )
    pl.when(me > 0)(upward.start)
    pl.when(me < n - 1)(downward.start)

    @pl.when(me == 0)
    def _():
        skip_planes[:edge] = jnp.zeros((edge, plane), skip_planes.dtype)

    @pl.when(me == n - 1)
    def _():
        skip_planes[(MARGIN + own) * skipc :] = jnp.zeros((edge, plane), skip_planes.dtype)

    at = iota((plane, 1), 0)
    z, x = lax.div(at, fine_w), lax.rem(at, fine_w)
    w = lax.div(x, 2)
    taken = lax.div(w, local_w) * slab + lax.div(z, 2) * local_w + lax.rem(w, local_w)
    parity = lax.rem(z, 2) * 2 + lax.rem(x, 2)

    def fill_source(h, _):
        rows_at(source, h, plane)[...] = one_hot(taken + h * (depth * local_w), n * slab)

    for i in range(near + 2):
        fill_source(i, None)

    chunk = fine_d * own

    def fill_order(o, _):
        rows_at(order, o, chunk)[...] = one_hot(iota((chunk, 1), 0) * outc + o, chunk * outc)

    lax.fori_loop(0, outc, fill_order, None)

    for load in loads[2:]:
        load.wait()
    for b in range(2):
        pieces = [(((a * 2 + b) * 2 + c) * cup, cup) for a in range(2) for c in range(2)]
        up_stack[b * cup : (b + 1) * cup] = stack_taps(upw_ref, pieces, slice(None))
    block = 3 * outc
    for p in range(3):
        pieces = [((p * 3 + q) * block, block) for q in range(3)]
        rows = slice(p * block, (p + 1) * block)
        up1[rows] = stack_taps(w1_ref, pieces, slice(0, cup))
        skip1[rows] = stack_taps(w1_ref, pieces, slice(cup, cup + skipc))
        stack2[rows] = stack_taps(w2_ref, pieces, slice(None))
    up_bias, bias1, bias2 = column(upb_ref[...]), column(b1_ref[...]), column(b2_ref[...])
    up_bias = jnp.concatenate([up_bias, up_bias], axis=0)

    def inside(row):
        return (me * own + row >= 0) & (me * own + row < n * own)

    pl.when(me < n - 1)(upward.wait_recv)
    pl.when(me > 0)(downward.wait_recv)

    def convolve_skip(t, _):
        rows_at(partial, t, 9 * outc)[...] = nn_dot(skip1[...], rows_at(skip_planes, t, skipc, 3 * skipc)[...])

    for i in range(own + 2):
        convolve_skip(i, None)
    pltpu.make_async_copy(incoming, incoming, coarse_recv).wait()

    received = incoming[...].reshape(n * slab, 2 * cup)
    received = jnp.concatenate([received] * 2, axis=1)
    mine = parity == lax.div(iota((1, 4 * cup), 1), cup)

    def upsample_row(h, _):
        spread = nn_dot(rows_at(source, h, plane)[...], received)
        spread = jnp.where(mine, spread, 0.0).astype(jnp.bfloat16)
        values = nt_dot(up_stack[...], spread) + up_bias
        values = jnp.where(inside(2 * h - MARGIN), values, 0.0)
        rows_at(up_planes, h, 2 * cup)[...] = values.astype(jnp.bfloat16)

    for i in range(near + 2):
        upsample_row(i, None)

    def convolve_joined(t, _):
        taps = nn_dot(up1[...], rows_at(up_planes, t, cup, 3 * cup)[...]) + rows_at(partial, t, 9 * outc)[...]
        values = jnp.maximum(moved_sum(taps, fine_w, fine_d, outc) + bias1, 0.0)
        values = jnp.where(inside(t - 1), values, 0.0)
        rows_at(hidden, t, outc)[...] = values.astype(jnp.bfloat16)

    for i in range(own + 2):
        convolve_joined(i, None)

    def convolve_hidden(t, _):
        taps = nn_dot(stack2[...], rows_at(hidden, t, outc, 3 * outc)[...])
        values = jnp.maximum(moved_sum(taps, fine_w, fine_d, outc) + bias2, 0.0)
        rows_at(outs, t, outc)[...] = values.astype(jnp.bfloat16)

    for i in range(own):
        convolve_hidden(i, None)
    slices = [outs[:, z * fine_w : (z + 1) * fine_w] for z in range(fine_d)]
    out_ref[...] = nn_dot(order[...], jnp.concatenate(slices, axis=0)).astype(jnp.bfloat16)

    pl.when(me > 0)(upward.wait_send)
    pl.when(me < n - 1)(downward.wait_send)
    pltpu.make_async_copy(outgoing.at[pl.ds(0, n - 1)], incoming.at[pl.ds(0, n - 1)], coarse_send).wait()


def body(coarse, skip, up_weight, up_bias, conv1_weight, conv1_bias, conv2_weight, conv2_bias):
    n = lax.axis_size("ha")
    cup, depth, local_w, height = coarse.shape
    skipc, fine_d, own, fine_w = skip.shape
    outc = conv1_weight.shape[3]
    near = height // n
    width = local_w * n
    plane = fine_d * fine_w
    slab = -(-((near + 2) * depth * local_w) // ROW_TILE) * ROW_TILE
    need = (near + 2) * plane * (n * slab * 6 + 4 * 8 * cup) + (own + 4) * 27 * outc * plane * 4
    if need > VMEM_BUDGET or plane % 128 or near < 1 or own < MARGIN:
        return large_body(
            coarse, skip, up_weight, up_bias, conv1_weight, conv1_bias, conv2_weight, conv2_bias
        )
    reach = own + 2 * MARGIN
    operands = (
        jnp.transpose(coarse, (1, 2, 3, 0)).reshape(depth * local_w * height, cup),
        skip.reshape(skipc * fine_d * own, fine_w),
        up_weight.reshape(8 * cup, cup),
        up_bias[None],
        conv1_weight.reshape(27 * outc, cup + skipc),
        conv1_bias[None],
        conv2_weight.reshape(27 * outc, outc),
        conv2_bias[None],
    )
    out = pl.pallas_call(
        functools.partial(kernel, n, depth, width, height, slab),
        out_shape=pltpu.VMEM((outc * fine_d * own, fine_w), jnp.bfloat16),
        in_specs=[pl.BlockSpec(memory_space=pltpu.HBM)] * len(operands),
        out_specs=pl.BlockSpec(memory_space=pltpu.VMEM),
        scratch_shapes=[pltpu.VMEM(operand.shape, operand.dtype) for operand in operands]
        + [
            pltpu.VMEM((n, slab, 2 * cup), jnp.bfloat16),
            pltpu.VMEM((n, slab, 2 * cup), jnp.bfloat16),
            pltpu.VMEM((reach * cup, plane), jnp.bfloat16),
            pltpu.VMEM((reach * skipc, plane), jnp.bfloat16),
            pltpu.VMEM(((own + 2) * outc, plane), jnp.bfloat16),
            pltpu.VMEM((own * outc, plane), jnp.bfloat16),
            pltpu.VMEM(((near + 2) * plane, n * slab), jnp.bfloat16),
            pltpu.VMEM((outc * fine_d * own, outc * fine_d * own), jnp.bfloat16),
            pltpu.VMEM((2 * cup, 4 * cup), jnp.bfloat16),
            pltpu.VMEM((9 * outc, 3 * cup), jnp.bfloat16),
            pltpu.VMEM((9 * outc, 3 * skipc), jnp.bfloat16),
            pltpu.VMEM((9 * outc, 3 * outc), jnp.bfloat16),
            pltpu.VMEM(((own + 2) * 9 * outc, plane), jnp.float32),
            pltpu.SemaphoreType.DMA,
            pltpu.SemaphoreType.DMA,
            pltpu.SemaphoreType.DMA((2,)),
            pltpu.SemaphoreType.DMA((2,)),
            pltpu.SemaphoreType.DMA((len(operands),)),
        ],
        compiler_params=pltpu.CompilerParams(
            collective_id=0, has_side_effects=True, vmem_limit_bytes=VMEM_LIMIT
        ),
    )(*(pltpu.with_memory_space_constraint(operand, pltpu.HBM) for operand in operands))
    return out.reshape(outc, fine_d, own, fine_w)


def solution(mesh):
    return jax.shard_map(
        body,
        mesh=mesh,
        in_specs=(
            P(None, "groups", "ha", None),
            P(None, "groups", "ha", None),
            P(),
            P(),
            P(),
            P(),
            P(),
            P(),
        ),
        out_specs=P(None, "groups", "ha", None),
        check_vma=False,
    )
```

```python
import functools

import jax
import jax.numpy as jnp
from jax import lax
from jax.experimental import pallas as pl
from jax.experimental.pallas import tpu as pltpu
from jax.sharding import PartitionSpec as P

VMEM_BUDGET = 40 * 1024 * 1024
VMEM_LIMIT = 48 * 1024 * 1024
MARGIN = 2
ROW_TILE = 16


def with_halo(array, sides, width):
    for axis, dim in sides:
        count, length = (lax.axis_size(axis), array.shape[dim])
        up = [(i, (i + 1) % count) for i in range(count - 1)]
        down = [(j, i) for i, j in up]
        last = lax.slice_in_dim(array, length - width, length, axis=dim)
        first = lax.slice_in_dim(array, 0, width, axis=dim)
        before = lax.ppermute(last, axis, up)
        after = lax.ppermute(first, axis, down)
        array = jnp.concatenate([before, array, after], axis=dim)
    return array


def upsample(inputs, weight, bias):
    values = jnp.einsum("abcoi,idpq->odapbqc", weight, inputs, preferred_element_type=jnp.float32)
    channels = weight.shape[3]
    values = values.reshape(channels, 2 * inputs.shape[1], 2 * inputs.shape[2], 2 * inputs.shape[3])
    return (values + bias[:, None, None, None]).astype(jnp.bfloat16)


def convolve(inputs, weight, bias):
    result = lax.conv_general_dilated(
        inputs[None],
        weight,
        (1, 1, 1),
        ((1, 1), (0, 0), (1, 1)),
        dimension_numbers=("NCDHW", "DHWOI", "NCDHW"),
        preferred_element_type=jnp.float32,
    )[0]
    return jnp.maximum(result + bias[:, None, None, None], 0.0).astype(jnp.bfloat16)


def inside_rows(height_rows, margin_rows):
    row_index = (
        lax.axis_index("ha") * height_rows
        - margin_rows
        + jnp.arange(height_rows + 2 * margin_rows, dtype=jnp.int32)
    )
    return (row_index >= 0) & (row_index < lax.axis_size("ha") * height_rows)


def large_body(coarse, skip, up_weight, up_bias, conv1_weight, conv1_bias, conv2_weight, conv2_bias):
    margin_rows = 2
    height_rows = skip.shape[2]
    local_fine = upsample(coarse, jnp.transpose(up_weight, (0, 2, 1, 3, 4)), up_bias)
    moved = lax.all_to_all(local_fine, "ha", split_axis=3, concat_axis=2, tiled=True)
    joined = jnp.concatenate([jnp.swapaxes(moved, 2, 3), skip], axis=0)
    padded = with_halo(joined, (("ha", 2),), margin_rows)
    widened = convolve(padded, conv1_weight, conv1_bias)
    inside = inside_rows(height_rows, 1)
    padded_hidden = jnp.where(inside[None, None, :, None], widened, jnp.zeros((), jnp.bfloat16))
    return convolve(padded_hidden, conv2_weight, conv2_bias)


def iota(shape, dim):
    return lax.broadcasted_iota(jnp.int32, shape, dim)


def column(row):
    size = row.shape[1]
    same = iota((size, size), 0) == iota((size, size), 1)
    return jnp.sum(jnp.where(same, row, 0.0), axis=1, keepdims=True)


def as_bits(mask):
    return jnp.where(mask, 1.0, 0.0).astype(jnp.bfloat16)


def one_hot(wanted, count):
    return as_bits(iota((wanted.shape[0], count), 1) == wanted)


def nt_dot(a, b):
    return lax.dot_general(a, b, (((1,), (1,)), ((), ())), preferred_element_type=jnp.float32)


def nn_dot(a, b):
    return lax.dot_general(a, b, (((1,), (0,)), ((), ())), preferred_element_type=jnp.float32)


def same_depth(channels, own, fine_d, fine_w):
    row = iota((channels * fine_d * own, 1), 0)
    lane = iota((1, fine_d * fine_w), 1)
    return lax.rem(lax.div(row, own), fine_d) == lax.div(lane, fine_w)


def width_tiles(fine_d, fine_w):
    shape = (fine_w, fine_d * fine_w)
    return as_bits(lax.rem(iota(shape, 1), fine_w) == iota(shape, 0))


def planes_of(rows, channels, own, fine_d, fine_w):
    wide = nn_dot(rows, width_tiles(fine_d, fine_w))
    wide = jnp.where(same_depth(channels, own, fine_d, fine_w), wide, 0.0).astype(jnp.bfloat16)
    at = iota((1, rows.shape[0]), 1)
    goal = lax.rem(at, own) * channels + lax.div(at, own * fine_d)
    return nn_dot(as_bits(iota((own * channels, 1), 0) == goal), wide).astype(jnp.bfloat16)


def stack_taps(weights, pieces, lanes):
    return jnp.concatenate([weights[at : at + size, lanes] for at, size in pieces], axis=1)


def moved_sum(taps, fine_w, fine_d, outc):
    plane = fine_w * fine_d
    lane = iota((1, plane), 1)
    x, z = lax.rem(lane, fine_w), lax.div(lane, fine_w)
    planes = []
    for p in range(3):
        before, here, after = (taps[(p * 3 + r) * outc : (p * 3 + r + 1) * outc] for r in range(3))
        here = here + jnp.where(x > 0, pltpu.roll(before, 1, 1), 0.0)
        here = here + jnp.where(x < fine_w - 1, pltpu.roll(after, plane - 1, 1), 0.0)
        planes.append(here)
    total = planes[1]
    total = total + jnp.where(z > 0, pltpu.roll(planes[0], fine_w, 1), 0.0)
    return total + jnp.where(z < fine_d - 1, pltpu.roll(planes[2], plane - fine_w, 1), 0.0)


def rows_at(ref, index, size, count=None):
    first = index * size if isinstance(index, int) else pl.multiple_of(index * size, size)
    return ref.at[pl.ds(first, size if count is None else count)]


def kernel(
    n, depth, width, height, slab,
    coarse_hbm, skip_hbm, upw_hbm, upb_hbm, w1_hbm, b1_hbm, w2_hbm, b2_hbm,
    out_ref,
    coarse_ref, skip_ref, upw_ref, upb_ref, w1_ref, b1_ref, w2_ref, b2_ref,
    outgoing, incoming, up_planes, skip_planes, hidden, source, up_stack, up1, skip1, stack2, partial,
    coarse_send, coarse_recv, skip_send, skip_recv, load_sem,
):
    me = lax.axis_index("ha")
    cup, outc = upw_ref.shape[1], w2_ref.shape[1]
    skipc = w1_ref.shape[1] - cup
    near = height // n
    own = 2 * near
    local_w = width // n
    fine_w, fine_d = 2 * width, 2 * depth
    plane = fine_w * fine_d
    reach = own + 2 * MARGIN

    operands = (
        (coarse_hbm, coarse_ref), (skip_hbm, skip_ref), (w1_hbm, w1_ref), (w2_hbm, w2_ref),
        (upw_hbm, upw_ref), (upb_hbm, upb_ref), (b1_hbm, b1_ref), (b2_hbm, b2_ref),
    )
    loads = [pltpu.make_async_copy(src, dst, load_sem.at[i]) for i, (src, dst) in enumerate(operands)]
    for load in loads[:2]:
        load.start()
    barrier = pltpu.get_barrier_semaphore()
    for k in range(1, n):
        pl.semaphore_signal(
            barrier, inc=1, device_id={"ha": lax.rem(me + k, n)}, device_id_type=pl.DeviceIdType.MESH
        )
    for load in loads[2:]:
        load.start()

    at = iota((n * slab, 1), 0)
    to, slot = lax.div(at, slab), lax.rem(at, slab)
    row = to * near - 1 + lax.div(slot, depth * local_w)
    wanted = (lax.rem(lax.div(slot, local_w), depth) * local_w + lax.rem(slot, local_w)) * height + row
    real = (row >= 0) & (row < height) & (slot < (near + 2) * depth * local_w)
    pick = one_hot(jnp.where(real, wanted, -1), depth * local_w * height)
    loads[0].wait()
    twice = jnp.concatenate([coarse_ref[...]] * 2, axis=1)
    outgoing[...] = nn_dot(pick, twice).astype(jnp.bfloat16).reshape(n, slab, 2 * cup)
    pl.semaphore_wait(barrier, n - 1)

    for k in range(1, n):
        to = lax.rem(me + (n // 2 + k - 1) % (n - 1) + 1, n)
        pltpu.make_async_remote_copy(
            src_ref=outgoing.at[to], dst_ref=incoming.at[me],
            send_sem=coarse_send, recv_sem=coarse_recv,
            device_id={"ha": to}, device_id_type=pl.DeviceIdType.MESH,
        ).start()
    pltpu.make_async_copy(outgoing.at[me], incoming.at[me], coarse_recv).start()

    edge = MARGIN * skipc
    loads[1].wait()
    skip_planes[edge : edge + own * skipc] = planes_of(skip_ref[...], skipc, own, fine_d, fine_w)
    upward = pltpu.make_async_remote_copy(
        src_ref=skip_planes.at[pl.ds(edge, edge)], dst_ref=skip_planes.at[pl.ds((MARGIN + own) * skipc, edge)],
        send_sem=skip_send.at[0], recv_sem=skip_recv.at[0],
        device_id={"ha": jnp.maximum(me - 1, 0)}, device_id_type=pl.DeviceIdType.MESH,
    )
    downward = pltpu.make_async_remote_copy(
        src_ref=skip_planes.at[pl.ds(own * skipc, edge)], dst_ref=skip_planes.at[pl.ds(0, edge)],
        send_sem=skip_send.at[1], recv_sem=skip_recv.at[1],
        device_id={"ha": jnp.minimum(me + 1, n - 1)}, device_id_type=pl.DeviceIdType.MESH,
    )
    pl.when(me > 0)(upward.start)
    pl.when(me < n - 1)(downward.start)

    @pl.when(me == 0)
    def _():
        skip_planes[:edge] = jnp.zeros((edge, plane), skip_planes.dtype)

    @pl.when(me == n - 1)
    def _():
        skip_planes[(MARGIN + own) * skipc :] = jnp.zeros((edge, plane), skip_planes.dtype)

    at = iota((plane, 1), 0)
    z, x = lax.div(at, fine_w), lax.rem(at, fine_w)
    w = lax.div(x, 2)
    taken = lax.div(w, local_w) * slab + lax.div(z, 2) * local_w + lax.rem(w, local_w)
    parity = lax.rem(z, 2) * 2 + lax.rem(x, 2)

    def fill_source(h, _):
        rows_at(source, h, plane)[...] = one_hot(taken + h * (depth * local_w), n * slab)

    for i in range(near + 2):
        fill_source(i, None)

    for load in loads[2:]:
        load.wait()
    for b in range(2):
        pieces = [(((a * 2 + b) * 2 + c) * cup, cup) for a in range(2) for c in range(2)]
        up_stack[b * cup : (b + 1) * cup] = stack_taps(upw_ref, pieces, slice(None))
    block = 3 * outc
    for p in range(3):
        pieces = [((p * 3 + q) * block, block) for q in range(3)]
        rows = slice(p * block, (p + 1) * block)
        up1[rows] = stack_taps(w1_ref, pieces, slice(0, cup))
        skip1[rows] = stack_taps(w1_ref, pieces, slice(cup, cup + skipc))
        stack2[rows] = stack_taps(w2_ref, pieces, slice(None))
    up_bias, bias1, bias2 = column(upb_ref[...]), column(b1_ref[...]), column(b2_ref[...])
    up_bias = jnp.concatenate([up_bias, up_bias], axis=0)

    def inside(row):
        return (me * own + row >= 0) & (me * own + row < n * own)

    pl.when(me < n - 1)(upward.wait_recv)
    pl.when(me > 0)(downward.wait_recv)

    def convolve_skip(t, _):
        rows_at(partial, t, 9 * outc)[...] = nn_dot(skip1[...], rows_at(skip_planes, t, skipc, 3 * skipc)[...])

    for i in range(own + 2):
        convolve_skip(i, None)
    pltpu.make_async_copy(incoming, incoming, coarse_recv).wait()

    received = incoming[...].reshape(n * slab, 2 * cup)
    received = jnp.concatenate([received] * 2, axis=1)
    mine = parity == lax.div(iota((1, 4 * cup), 1), cup)

    def upsample_row(h, _):
        spread = nn_dot(rows_at(source, h, plane)[...], received)
        spread = jnp.where(mine, spread, 0.0).astype(jnp.bfloat16)
        values = nt_dot(up_stack[...], spread) + up_bias
        values = jnp.where(inside(2 * h - MARGIN), values, 0.0)
        rows_at(up_planes, h, 2 * cup)[...] = values.astype(jnp.bfloat16)

    for i in range(near + 2):
        upsample_row(i, None)

    def convolve_joined(t, _):
        taps = nn_dot(up1[...], rows_at(up_planes, t, cup, 3 * cup)[...]) + rows_at(partial, t, 9 * outc)[...]
        values = jnp.maximum(moved_sum(taps, fine_w, fine_d, outc) + bias1, 0.0)
        values = jnp.where(inside(t - 1), values, 0.0)
        rows_at(hidden, t, outc)[...] = values.astype(jnp.bfloat16)

    for i in range(own + 2):
        convolve_joined(i, None)

    def convolve_hidden(t, _):
        taps = nn_dot(stack2[...], rows_at(hidden, t, outc, 3 * outc)[...])
        values = jnp.maximum(moved_sum(taps, fine_w, fine_d, outc) + bias2, 0.0)
        out_ref[:, t * plane : (t + 1) * plane] = values.astype(jnp.bfloat16)

    for i in range(own):
        convolve_hidden(i, None)

    pl.when(me > 0)(upward.wait_send)
    pl.when(me < n - 1)(downward.wait_send)
    pltpu.make_async_copy(outgoing.at[pl.ds(0, n - 1)], incoming.at[pl.ds(0, n - 1)], coarse_send).wait()


def body(coarse, skip, up_weight, up_bias, conv1_weight, conv1_bias, conv2_weight, conv2_bias):
    n = lax.axis_size("ha")
    cup, depth, local_w, height = coarse.shape
    skipc, fine_d, own, fine_w = skip.shape
    outc = conv1_weight.shape[3]
    near = height // n
    width = local_w * n
    plane = fine_d * fine_w
    slab = -(-((near + 2) * depth * local_w) // ROW_TILE) * ROW_TILE
    need = (near + 2) * plane * (n * slab * 6 + 4 * 8 * cup) + (own + 4) * 27 * outc * plane * 4
    if need > VMEM_BUDGET or plane % 128 or near < 1 or own < MARGIN:
        return large_body(
            coarse, skip, up_weight, up_bias, conv1_weight, conv1_bias, conv2_weight, conv2_bias
        )
    reach = own + 2 * MARGIN
    operands = (
        jnp.transpose(coarse, (1, 2, 3, 0)).reshape(depth * local_w * height, cup),
        skip.reshape(skipc * fine_d * own, fine_w),
        up_weight.reshape(8 * cup, cup),
        up_bias[None],
        conv1_weight.reshape(27 * outc, cup + skipc),
        conv1_bias[None],
        conv2_weight.reshape(27 * outc, outc),
        conv2_bias[None],
    )
    out = pl.pallas_call(
        functools.partial(kernel, n, depth, width, height, slab),
        out_shape=pltpu.VMEM((outc, own * plane), jnp.bfloat16),
        in_specs=[pl.BlockSpec(memory_space=pltpu.HBM)] * len(operands),
        out_specs=pl.BlockSpec(memory_space=pltpu.VMEM),
        scratch_shapes=[pltpu.VMEM(operand.shape, operand.dtype) for operand in operands]
        + [
            pltpu.VMEM((n, slab, 2 * cup), jnp.bfloat16),
            pltpu.VMEM((n, slab, 2 * cup), jnp.bfloat16),
            pltpu.VMEM((reach * cup, plane), jnp.bfloat16),
            pltpu.VMEM((reach * skipc, plane), jnp.bfloat16),
            pltpu.VMEM(((own + 2) * outc, plane), jnp.bfloat16),
            pltpu.VMEM(((near + 2) * plane, n * slab), jnp.bfloat16),
            pltpu.VMEM((2 * cup, 4 * cup), jnp.bfloat16),
            pltpu.VMEM((9 * outc, 3 * cup), jnp.bfloat16),
            pltpu.VMEM((9 * outc, 3 * skipc), jnp.bfloat16),
            pltpu.VMEM((9 * outc, 3 * outc), jnp.bfloat16),
            pltpu.VMEM(((own + 2) * 9 * outc, plane), jnp.float32),
            pltpu.SemaphoreType.DMA,
            pltpu.SemaphoreType.DMA,
            pltpu.SemaphoreType.DMA((2,)),
            pltpu.SemaphoreType.DMA((2,)),
            pltpu.SemaphoreType.DMA((len(operands),)),
        ],
        compiler_params=pltpu.CompilerParams(
            collective_id=0, has_side_effects=True, vmem_limit_bytes=VMEM_LIMIT
        ),
    )(*(pltpu.with_memory_space_constraint(operand, pltpu.HBM) for operand in operands))
    return jnp.swapaxes(out.reshape(outc, own, fine_d, fine_w), 1, 2)


def solution(mesh):
    return jax.shard_map(
        body,
        mesh=mesh,
        in_specs=(
            P(None, "groups", "ha", None),
            P(None, "groups", "ha", None),
            P(),
            P(),
            P(),
            P(),
            P(),
            P(),
        ),
        out_specs=P(None, "groups", "ha", None),
        check_vma=False,
    )
```
